256 devices in a mesh: section: 16 (over x_lo, y, core), expert: 16 (over z, x_hi).
Axes of the slice: x: 4 (x_hi: 2, x_lo: 2; x = x_hi * 2 + x_lo), y: 4, z: 8, core: 2. Of those that a mesh axis runs over, the one named last changes fastest.
Arguments:
- activations: bfloat16 [16, 2048, 4096], P('section', 'expert'), may hold values from -6 to 6
- norm_gain: bfloat16 [16, 4096], P('section'), may hold values from 0.099609375 to 1.8984375
- w_gate: bfloat16 [16, 4096, 6144], P('section', None, 'expert'), may hold values from -0.09375 to 0.09375
- w_up: bfloat16 [16, 4096, 6144], P('section', None, 'expert'), may hold values from -0.09375 to 0.09375
- w_down: bfloat16 [16, 6144, 4096], P('section', 'expert'), may hold values from -0.15625 to 0.15625
- expert_ids: int32 [2, 16, 2048, 8], P(None, 'section', 'expert'), may hold values from 0 to 127, as said below
- route_weights: float32 [2, 16, 2048, 8], P(None, 'section', 'expert'), may hold values from 0.5 to 2
Outputs:
- final_state: bfloat16 [16, 2048, 4096], P('section', 'expert')
The draws below stay inside these ranges and needn't reach their ends.
Inputs may be any that keep to these rules, and one draw needn't show every extreme that they name: `expert_ids`: each token names 8 different experts. In every aligned block of 128 tokens (one device's tokens), at every stop and section, each expert below 4 is named by at most 16 tokens, and at every stop and section one of them is named by exactly 16 tokens in every block.
All inputs are finite; a program needn't handle non-finite values.
Results may differ from the reference program's by a relative error of at most 0.007.
Values may be sent and summed in bfloat16 or wider, within the bound.
A program may use at most 64 MiB of HBM per device.

```python
import math
import jax
import jax.numpy as jnp
from jax import lax

D = 4096
FF = 1536
SPECIALIST_TOTAL = 128
TOP = 8
SPECIALIST_SPAN = 4
HANDOFF_PASSES = 2
T_DEV = 128
SEGMENT_TALLY = 16
SUBBATCH_ITEMS = 2048


def draw_expert_ids(key, part):
    key = jax.random.fold_in(key, 7)
    key_offset, key_hot, key_coin, key_rest, key_order = jax.random.split(key, 5)
    blocks = SUBBATCH_ITEMS // T_DEV
    capacity = T_DEV // 8
    offsets = jax.random.randint(key_offset, (HANDOFF_PASSES, SEGMENT_TALLY, blocks, 1, SPECIALIST_SPAN), 0, T_DEV)
    hot_expert = jax.random.randint(key_hot, (HANDOFF_PASSES, SEGMENT_TALLY, 1, 1, 1), 0, SPECIALIST_SPAN)
    token_place = jnp.arange(T_DEV, dtype=jnp.int32)[:, None]
    allowed = jnp.mod(token_place - offsets, T_DEV) < capacity
    coin_flip = jax.random.randint(key_coin, allowed.shape, 0, 3) == 0
    is_hot = jnp.arange(SPECIALIST_SPAN, dtype=jnp.int32) == hot_expert
    chosen = jnp.logical_and(allowed, jnp.logical_or(is_hot, coin_flip))
    chosen = chosen.reshape(HANDOFF_PASSES, SEGMENT_TALLY, SUBBATCH_ITEMS, SPECIALIST_SPAN)
    rest_scores = jax.random.randint(key_rest, (HANDOFF_PASSES, SEGMENT_TALLY, SUBBATCH_ITEMS, SPECIALIST_TOTAL), 0, 65536)
    column = jnp.arange(SPECIALIST_TOTAL, dtype=jnp.int32)
    gating_raw_scores = rest_scores * SPECIALIST_TOTAL + column
    visible_fraction = jnp.where(chosen, 1 << 26, -(1 << 26)).astype(jnp.int32)
    extra_added_shift = jnp.concatenate([visible_fraction, jnp.zeros((HANDOFF_PASSES, SEGMENT_TALLY, SUBBATCH_ITEMS, SPECIALIST_TOTAL - SPECIALIST_SPAN), jnp.int32)], axis=-1)
    gating_raw_scores = gating_raw_scores + extra_added_shift
    picked = lax.top_k(gating_raw_scores, TOP)[1]
    order_keys = jax.random.randint(key_order, picked.shape, 0, 4096) * TOP + jnp.arange(TOP, dtype=jnp.int32)
    permute = jnp.argsort(order_keys, axis=-1)
    return jnp.take_along_axis(picked, permute, axis=-1).astype(jnp.int32)


def block_scale(rng, dims, pieces, smallest, high):
    factor_of = 1.0
    for dim, blocks in pieces:
        steps = jax.random.uniform(jax.random.fold_in(jax.random.fold_in(rng, 6), dim), (blocks,), jnp.float32, smallest / len(pieces), high / len(pieces))
        factor_of = factor_of * jnp.repeat(jnp.exp(steps), dims[dim] // blocks).reshape((-1,) + (1,) * (len(dims) - 1 - dim))
    return factor_of


def gaussian(own_key, shape, spread, limit, pieces=(), kind=jnp.bfloat16):
    gain = block_scale(own_key, shape, pieces, -0.22, 0.18) if pieces else 1.0
    array = jax.random.normal(own_key, shape, jnp.float32) * spread * gain
    return jnp.minimum(jnp.maximum(array, -limit), limit).astype(kind)


def setup_inputs(seed: int = 0) -> dict:
    keys = jax.random.split(jax.random.key(seed), 8)
    activations = gaussian(keys[0], (SEGMENT_TALLY, SUBBATCH_ITEMS, D), 1.0, 6.0, ((0, 16), (1, 16)))
    norm_gain = jnp.clip(1.0 + 0.18 * jax.random.normal(keys[1], (SEGMENT_TALLY, D), jnp.float32), 0.099609375, 1.8984375).astype(jnp.bfloat16)
    w_gate = gaussian(keys[2], (SEGMENT_TALLY, D, SPECIALIST_SPAN * FF), D ** -0.5, 0.09375, ((0, 16), (2, 16)))
    w_up = gaussian(keys[3], (SEGMENT_TALLY, D, SPECIALIST_SPAN * FF), D ** -0.5, 0.09375, ((0, 16), (2, 16)))
    w_down = gaussian(keys[4], (SEGMENT_TALLY, SPECIALIST_SPAN * FF, D), FF ** -0.5, 0.15625, ((0, 16), (1, 16)))
    expert_ids = draw_expert_ids(jax.random.fold_in(keys[7], 71), 0)
    route_weights = jnp.clip(jnp.exp(math.log(2.0) - 1.3862944 * jax.random.uniform(keys[6], (HANDOFF_PASSES, SEGMENT_TALLY, SUBBATCH_ITEMS, TOP), jnp.float32) ** block_scale(keys[6], (HANDOFF_PASSES, SEGMENT_TALLY, SUBBATCH_ITEMS, TOP), ((1, 16), (2, 16)), -0.2, 0.2)), 0.5, 2.0)
    return dict(activations=activations, norm_gain=norm_gain, w_gate=w_gate, w_up=w_up, w_down=w_down, expert_ids=expert_ids, route_weights=route_weights)


def root_norm(values, norm_gain):
    as_float = values.astype(jnp.float32)
    scale_factor = lax.rsqrt(lax.optimization_barrier(jnp.mean(as_float * as_float, axis=-1, keepdims=True)) + 1e-06)
    return (as_float * scale_factor * norm_gain.astype(jnp.float32)).astype(jnp.bfloat16)

def apply_layer(carried, norm_gain, w_gate, w_up, w_down, expert_ids, route_weights):
    count = carried.shape[0]
    blocks = count // T_DEV
    capacity = T_DEV // 8
    normed = root_norm(carried, norm_gain)
    total = carried.astype(jnp.float32)
    for expert in range(SPECIALIST_SPAN):
        is_named = expert_ids == expert
        matched = jnp.any(is_named, axis=-1)
        factor = lax.optimization_barrier(jnp.sum(jnp.where(is_named, route_weights, 0.0), axis=-1))
        slot_rank = jnp.cumsum(matched.reshape(blocks, T_DEV).astype(jnp.int32), axis=1) - 1
        slot_pos = (jnp.arange(blocks, dtype=jnp.int32)[:, None] * capacity + slot_rank).reshape(-1).astype(jnp.int32)
        target = jnp.where(matched, slot_pos, blocks * capacity).astype(jnp.int32)
        source = jnp.zeros((blocks * capacity + 1,), jnp.int32).at[target].set(jnp.arange(count, dtype=jnp.int32))
        filled = jnp.zeros((blocks * capacity + 1,), jnp.int32).at[target].set(1)
        slot_rows = jnp.where(filled[:-1, None] == 1, normed[source[:-1]], jnp.zeros((), jnp.bfloat16))
        columns = slice(expert * FF, (expert + 1) * FF)
        gate_act = jnp.dot(slot_rows, w_gate[:, columns], preferred_element_type=jnp.float32)
        up_act = jnp.dot(slot_rows, w_up[:, columns], preferred_element_type=jnp.float32)
        hidden = (jax.nn.silu(gate_act) * up_act).astype(jnp.bfloat16)
        expert_out = jnp.dot(hidden, w_down[columns, :], preferred_element_type=jnp.float32).astype(jnp.bfloat16)
        gathered = expert_out[jnp.minimum(target, blocks * capacity - 1)].astype(jnp.float32)
        total = total + jnp.where(matched, factor, 0.0)[:, None] * gathered
    return total.astype(jnp.bfloat16)

def reference(activations, norm_gain, w_gate, w_up, w_down, expert_ids, route_weights):
    carried = activations
    for stop_index in range(HANDOFF_PASSES):

        def one_section(section_items):
            return apply_layer(*section_items)
        carried = lax.map(one_section, (carried, norm_gain, w_gate, w_up, w_down, expert_ids[stop_index], route_weights[stop_index]))
        if stop_index + 1 < HANDOFF_PASSES:
            carried = jnp.roll(carried, 1, axis=0)
    return carried
```

```python
import functools

import jax
import jax.numpy as jnp
from jax import lax
from jax.experimental import pallas as pl
from jax.experimental.pallas import tpu as pltpu
from jax.sharding import PartitionSpec as P

MESH = pl.DeviceIdType.MESH
F32, BF16 = jnp.float32, jnp.bfloat16
POS = {0: 0, 4: 1, 1: 2, 5: 3, 2: 4, 6: 5, 3: 6, 7: 7}
CAP = 16
UP, MATE, CROSS, BACK, PAIR, LAST = 0, 4, 8, 16, 24, 28
CHANNELS = 32


def unit(u):
    return pl.ds(POS[u] * CAP, CAP)


def routing(ids, weights, experts):
    tokens = ids.shape[1]
    matched, factors = [], []
    for e in experts:
        hit = ids == e
        matched.append(jnp.max(jnp.where(hit, 1.0, 0.0), axis=0, keepdims=True))
        factors.append(jnp.sum(jnp.where(hit, weights, 0.0), axis=0, keepdims=True))
    named = jnp.concatenate(matched + matched, axis=0)
    earlier = lax.broadcasted_iota(jnp.int32, (tokens, tokens), 0) < lax.broadcasted_iota(
        jnp.int32, (tokens, tokens), 1
    )
    rank = jnp.dot(
        named.astype(BF16), jnp.where(earlier, 1.0, 0.0).astype(BF16), preferred_element_type=F32
    )
    slot = lax.broadcasted_iota(jnp.int32, (CAP, tokens), 0).astype(F32)
    select = [
        jnp.where(jnp.logical_and(rank[j : j + 1] == slot, matched[j] > 0.5), 1.0, 0.0)
        for j in range(4)
    ]
    coefs = jnp.concatenate([select[j] * factors[j] for j in range(4)], axis=0)
    return jnp.concatenate(select, axis=0).astype(BF16), coefs


def split_coefs(coefs):
    first = coefs.astype(BF16).astype(F32)
    second = (coefs - first).astype(BF16).astype(F32)
    third = coefs - first - second
    left = jnp.concatenate([first, second], axis=0).T
    right = jnp.concatenate([third, jnp.zeros_like(third)], axis=0).T
    return jnp.concatenate([left, right], axis=1).astype(BF16)


def kernel(
    act, gain, wg, wu, wd, ids, weights, out,
    tok, sel, coef, rows, sbuf, own, par, gu, hid, psend, pown, rx, ms, rz, fs, res, w1, w2, pids, pwts,
    ssem, rsem, hs, hr, lsem,
):
    s, k = lax.axis_index("section"), lax.axis_index("expert")
    sections = lax.axis_size("section")
    z, h = k // 2, lax.rem(k, 2)
    b = lax.rem(z, 2)
    dr = 2 * b - 1
    p = z // 2
    width = tok.shape[2]
    hidden = wd.shape[0]
    nxt, prv = lax.rem(s + 1, sections), lax.rem(s + sections - 1, sections)

    def at(dz=0, cross=False, section=None):
        there = lax.rem(z + dz + 8, 8) * 2 + (1 - h if cross else h)
        return (s if section is None else section, there)

    loads = [
        pltpu.make_async_copy(act, tok.at[0], lsem.at[0]),
        pltpu.make_async_copy(wg, w1.at[:, pl.ds(0, hidden)], lsem.at[1]),
        pltpu.make_async_copy(wu, w1.at[:, pl.ds(hidden, hidden)], lsem.at[2]),
        pltpu.make_async_copy(wd, w2, lsem.at[3]),
    ]
    for load in loads:
        load.start()

    barrier = pltpu.get_barrier_semaphore()
    near = [at(dr), at(2 * dr), at(-2 * dr), at(3 * dr), at(-dr), at(0, cross=True)]
    below = [at(j, section=prv) for j in (0, dr, -2 * dr, 3 * dr)]
    for device in near + below:
        pl.semaphore_signal(barrier, inc=1, device_id=device, device_id_type=MESH)
    pl.semaphore_wait(barrier, len(near) + 4)

    def remote(src, dst, send, recv, device):
        return pltpu.make_async_remote_copy(
            src_ref=src, dst_ref=dst, send_sem=send, recv_sem=recv, device_id=device, device_id_type=MESH
        )

    handoff = [
        remote(ids.at[0], pids, hs.at[0], hr.at[0], at(section=nxt)),
        remote(weights.at[0], pwts, hs.at[1], hr.at[1], at(section=nxt)),
        remote(act, tok.at[1], hs.at[2], hr.at[2], at(section=nxt)),
    ]
    for copy in handoff:
        copy.start()

    experts = (p, lax.rem(p + dr + 4, 4), lax.rem(p - dr + 4, 4), lax.rem(p + 2, 4))
    sel[0] = routing(ids[0], weights[0], experts)[0]
    loads[0].wait()

    def prologue(r):
        def pick(n, total):
            cols = pl.ds(pl.multiple_of(n * 512, 512), 512)
            block = jnp.dot(sel[r], tok[2 * r, :, cols], preferred_element_type=F32)
            rows[:, cols] = block
            square = block * block
            return total + square[:, :128] + square[:, 128:256] + square[:, 256:384] + square[:, 384:]

        total = lax.fori_loop(0, width // 512, pick, jnp.zeros((4 * CAP, 128), F32))
        scale = lax.rsqrt(jnp.sum(total, axis=1, keepdims=True) * (1.0 / width) + 1e-06)

        @pl.loop(0, width // 512)
        def _(n):
            cols = pl.ds(pl.multiple_of(n * 512, 512), 512)
            block = (rows[:, cols] * scale * gain[:, cols].astype(F32)).astype(BF16)
            own[r, unit(0), cols] = block[:CAP]
            for j in range(1, 4):
                sbuf[r, j, :, cols] = block[j * CAP : (j + 1) * CAP]

    def epilogue(r, put):
        @pl.loop(0, width // 512)
        def _(n):
            cols = pl.ds(pl.multiple_of(n * 512, 512), 512)
            block = res[r, :, cols]
            mixed = jnp.dot(
                coef[r], jnp.concatenate([block] * 4, axis=0), preferred_element_type=F32
            )
            put(cols, (tok[1 + r, :, cols].astype(F32) + mixed).astype(BF16))

    def ffn(r, table, start, count, dst):
        chunk = pl.ds(start, count)

        @pl.loop(0, (2 * hidden) // 256)
        def _(n):
            cols = pl.ds(pl.multiple_of(n * 256, 256), 256)
            gu[pl.ds(0, count), cols] = jnp.dot(
                table[r, chunk, :], w1[:, cols], preferred_element_type=F32
            )

        gate, up = gu[pl.ds(0, count), pl.ds(0, hidden)], gu[pl.ds(0, count), pl.ds(hidden, hidden)]
        hid[pl.ds(0, count), :] = (gate / (1.0 + jnp.exp(-gate)) * up).astype(BF16)

        @pl.loop(0, width // 512)
        def _(n):
            cols = pl.ds(pl.multiple_of(n * 512, 512), 512)
            dst[r, chunk, cols] = jnp.dot(
                hid[pl.ds(0, count), :], w2[:, cols], preferred_element_type=F32
            ).astype(dst.dtype)

    started = []
    for r in range(2):

        def channel(src, dst, index, device):
            copy = remote(src, dst, ssem.at[r, index], rsem.at[r, index], device)
            return copy

        up = {
            j: channel(sbuf.at[r, j], own.at[r, unit(j)], UP + j, at(d))
            for j, d in ((1, dr), (2, -2 * dr), (3, 3 * dr))
        }
        mate = {
            j: channel(own.at[r, unit(j)], own.at[r, unit(4 + j)], MATE + j, at(-dr))
            for j in range(4)
        }
        cross = {
            u: channel(own.at[r, unit(u)], par.at[r, unit(u)], CROSS + u, at(0, cross=True))
            for u in range(8)
        }
        back = {
            u: channel(psend.at[r, unit(u)], rx.at[r, unit(u)], BACK + u, at(0, cross=True))
            for u in range(8)
        }
        pair = {
            j: channel(ms.at[r, j], rz.at[r, j], PAIR + j, at(-dr)) for j in range(4)
        }
        target = nxt if r == 0 else s
        last = {
            j: channel(
                fs.at[r, j],
                res.at[r, pl.ds(j * CAP, CAP)],
                LAST + j,
                at(dr * j, section=target),
            )
            for j in range(4)
            if r == 0 or j > 0
        }

        def go(copy):
            copy.start()
            started.append(copy)

        prologue(r)
        go(cross[0])
        go(mate[0])
        for j in (3, 2, 1):
            go(up[j])
        if r == 0:
            sel[1], coefs = routing(ids[1], weights[1], experts)
            coef[1] = split_coefs(coefs)
            handoff[0].wait_recv()
            handoff[1].wait_recv()
            coef[0] = split_coefs(routing(pids[...], pwts[...], experts)[1])
        for u in (4, 1, 5, 2, 6, 3, 7):
            if u < 4:
                up[u].wait_recv()
                go(mate[u])
            else:
                mate[u - 4].wait_recv()
            go(cross[u])
        if r == 0:
            for load in loads[1:]:
                load.wait()
        ffn(r, own, 0, 8 * CAP, pown)
        for half, order in ((0, (5, 4, 1, 0)), (1, (7, 6, 3, 2))):
            for u in order:
                cross[u].wait_recv()
            ffn(r, par, half * 4 * CAP, 4 * CAP, psend)
            for u in order:
                go(back[u])

        for first, second in ((1, 0), (3, 2)):
            for j in (first, second):
                back[4 + j].wait_recv()
                ms[r, j] = (pown[r, unit(4 + j), :] + rx[r, unit(4 + j), :].astype(F32)).astype(BF16)
                go(pair[j])
            for j in (first, second):
                back[j].wait_recv()
                pair[j].wait_recv()
                total = (
                    pown[r, unit(j), :] + rx[r, unit(j), :].astype(F32) + rz[r, j].astype(F32)
                ).astype(BF16)
                if j in last:
                    fs[r, j] = total
                    go(last[j])
                else:
                    res[r, pl.ds(j * CAP, CAP), :] = total
        for copy in last.values():
            copy.wait_recv()
        if r == 0:
            handoff[2].wait_recv()

            def keep(cols, block):
                tok[2, :, cols] = block
        else:

            def keep(cols, block):
                out[:, cols] = block

        epilogue(r, keep)

    for copy in started + handoff:
        copy.wait_send()


def body(activations, norm_gain, w_gate, w_up, w_down, expert_ids, route_weights):
    tokens, width = activations.shape[1:]
    hidden = w_gate.shape[2]
    slots = 4 * CAP
    anywhere = pl.BlockSpec(memory_space=pl.ANY)
    vmem = pl.BlockSpec(memory_space=pltpu.VMEM)
    out = pl.pallas_call(
        kernel,
        out_shape=jax.ShapeDtypeStruct((tokens, width), BF16),
        in_specs=[anywhere, vmem, anywhere, anywhere, anywhere, vmem, vmem],
        out_specs=vmem,
        scratch_shapes=[
            pltpu.VMEM((3, tokens, width), BF16),
            pltpu.VMEM((2, slots, tokens), BF16),
            pltpu.VMEM((2, tokens, 4 * slots), BF16),
            pltpu.VMEM((slots, width), F32),
            pltpu.VMEM((2, 4, CAP, width), BF16),
            pltpu.VMEM((2, 8 * CAP, width), BF16),
            pltpu.VMEM((2, 8 * CAP, width), BF16),
            pltpu.VMEM((8 * CAP, 2 * hidden), F32),
            pltpu.VMEM((8 * CAP, hidden), BF16),
            pltpu.VMEM((2, 8 * CAP, width), BF16),
            pltpu.VMEM((2, 8 * CAP, width), F32),
            pltpu.VMEM((2, 8 * CAP, width), BF16),
            pltpu.VMEM((2, 4, CAP, width), BF16),
            pltpu.VMEM((2, 4, CAP, width), BF16),
            pltpu.VMEM((2, 4, CAP, width), BF16),
            pltpu.VMEM((2, slots, width), BF16),
            pltpu.VMEM((width, 2 * hidden), BF16),
            pltpu.VMEM((hidden, width), BF16),
            pltpu.VMEM((8, tokens), jnp.int32),
            pltpu.VMEM((8, tokens), F32),
            pltpu.SemaphoreType.DMA((2, CHANNELS)),
            pltpu.SemaphoreType.DMA((2, CHANNELS)),
            pltpu.SemaphoreType.DMA((3,)),
            pltpu.SemaphoreType.DMA((3,)),
            pltpu.SemaphoreType.DMA((4,)),
        ],
        compiler_params=pltpu.CompilerParams(
            collective_id=0, has_side_effects=True, vmem_limit_bytes=56 << 20
        ),
        cost_estimate=pl.CostEstimate(
            flops=12 * 256 * width * hidden, bytes_accessed=12 << 20, transcendentals=512 * hidden
        ),
    )(
        activations[0],
        norm_gain,
        w_gate[0],
        w_up[0],
        w_down[0],
        jnp.swapaxes(expert_ids[:, 0], 1, 2),
        jnp.swapaxes(route_weights[:, 0], 1, 2),
    )
    return out[None]


def solution(mesh):
    return jax.shard_map(
        body,
        mesh=mesh,
        in_specs=(
            P("section", "expert", None),
            P("section", None),
            P("section", None, "expert"),
            P("section", None, "expert"),
            P("section", "expert", None),
            P(None, "section", "expert", None),
            P(None, "section", "expert", None),
        ),
        out_specs=P("section", "expert", None),
        check_vma=False,
    )
```

```python
import functools

import jax
import jax.numpy as jnp
from jax import lax
from jax.experimental import pallas as pl
from jax.experimental.pallas import tpu as pltpu
from jax.sharding import PartitionSpec as P

MESH = pl.DeviceIdType.MESH
F32, BF16 = jnp.float32, jnp.bfloat16
POS = {0: 0, 4: 1, 1: 2, 5: 3, 2: 4, 6: 5, 3: 6, 7: 7}
CAP = 16
UP, MATE, CROSS, BACK, PAIR, LAST = 0, 4, 8, 16, 24, 28
CHANNELS = 32


def unit(u):
    return pl.ds(POS[u] * CAP, CAP)


def routing(ids, weights, experts):
    tokens = ids.shape[1]
    matched, factors = [], []
    for e in experts:
        hit = ids == e
        matched.append(jnp.max(jnp.where(hit, 1.0, 0.0), axis=0, keepdims=True))
        factors.append(jnp.sum(jnp.where(hit, weights, 0.0), axis=0, keepdims=True))
    named = jnp.concatenate(matched + matched, axis=0)
    earlier = lax.broadcasted_iota(jnp.int32, (tokens, tokens), 0) < lax.broadcasted_iota(
        jnp.int32, (tokens, tokens), 1
    )
    rank = jnp.dot(
        named.astype(BF16), jnp.where(earlier, 1.0, 0.0).astype(BF16), preferred_element_type=F32
    )
    slot = lax.broadcasted_iota(jnp.int32, (CAP, tokens), 0).astype(F32)
    select = [
        jnp.where(jnp.logical_and(rank[j : j + 1] == slot, matched[j] > 0.5), 1.0, 0.0)
        for j in range(4)
    ]
    coefs = jnp.concatenate([select[j] * factors[j] for j in range(4)], axis=0)
    return jnp.concatenate(select, axis=0).astype(BF16), coefs


def split_coefs(coefs):
    first = coefs.astype(BF16).astype(F32)
    second = (coefs - first).astype(BF16).astype(F32)
    third = coefs - first - second
    left = jnp.concatenate([first, second], axis=0).T
    right = jnp.concatenate([third, jnp.zeros_like(third)], axis=0).T
    return jnp.concatenate([left, right], axis=1).astype(BF16)


def combine(coefs, results, carried):
    mixed = jnp.dot(coefs, jnp.concatenate([results] * 4, axis=0), preferred_element_type=F32)
    return (carried.astype(F32) + mixed).astype(BF16)


def last_step(coefs, results, carried, out, c, r, t, o, sems, osems):
    step = r.shape[2]
    loads = [pltpu.make_async_copy(coefs, c, sems.at[0])]
    for n in range(r.shape[0]):
        cols = pl.ds(n * step, step)
        loads.append(pltpu.make_async_copy(results.at[:, cols], r.at[n], sems.at[2 * n + 1]))
        loads.append(pltpu.make_async_copy(carried.at[:, cols], t.at[n], sems.at[2 * n + 2]))
    for load in loads:
        load.start()
    loads[0].wait()
    stores = []
    for n in range(r.shape[0]):
        loads[2 * n + 1].wait()
        loads[2 * n + 2].wait()
        o[n] = combine(c[...], r[n], t[n])
        stores.append(pltpu.make_async_copy(o.at[n], out.at[0, :, pl.ds(n * step, step)], osems.at[n]))
        stores[n].start()
    for store in stores:
        store.wait()


def kernel(
    act, gain, wg, wu, wd, ids, weights, base, results, coefs1,
    tok, sel, coef, rows, sbuf, own, par, gu, hid, psend, pown, rx, ms, rz, fs, res, w1, w2, pids, pwts,
    relay, ppr, ssem, rsem, hs, hr, lsem,
):
    s, k = lax.axis_index("section"), lax.axis_index("expert")
    sections = lax.axis_size("section")
    z, h = k // 2, lax.rem(k, 2)
    b = lax.rem(z, 2)
    dr = 2 * b - 1
    p = z // 2
    width = tok.shape[2]
    hidden = wd.shape[0]
    nxt, prv = lax.rem(s + 1, sections), lax.rem(s + sections - 1, sections)

    def at(dz=0, cross=False, section=None):
        there = lax.rem(z + dz + 8, 8) * 2 + (1 - h if cross else h)
        return (s if section is None else section, there)

    loads = [
        pltpu.make_async_copy(act, tok.at[0], lsem.at[0]),
        pltpu.make_async_copy(wg, w1.at[:, pl.ds(0, hidden)], lsem.at[1]),
        pltpu.make_async_copy(wu, w1.at[:, pl.ds(hidden, hidden)], lsem.at[2]),
        pltpu.make_async_copy(wd, w2, lsem.at[3]),
    ]
    for load in loads:
        load.start()
    keep_coefs = pltpu.make_async_copy(coef.at[1], coefs1, lsem.at[4])
    keep_base = pltpu.make_async_copy(tok.at[2], base, lsem.at[5])

    barrier = pltpu.get_barrier_semaphore()
    near = [at(dr), at(2 * dr), at(-2 * dr), at(3 * dr), at(-dr), at(0, cross=True)]
    below = [at(j, section=prv) for j in (0, dr, -2 * dr, 3 * dr)]
    for device in near + below:
        pl.semaphore_signal(barrier, inc=1, device_id=device, device_id_type=MESH)

    side, y, core = s // 8, lax.rem(s // 2, 4), lax.rem(s, 2)
    tail, head = side * 8 + 7, (1 - side) * 8
    is_tail = jnp.logical_and(y == 3, core == 1)
    is_head = jnp.logical_and(y == 0, core == 0)
    before = jnp.logical_and(y < 3, core == 1)
    after = jnp.logical_and(y > 0, core == 0)

    def greet(section):
        pl.semaphore_signal(barrier, inc=1, device_id=at(section=section), device_id_type=MESH)

    @pl.when(before)
    def _():
        greet(tail)

    @pl.when(after)
    def _():
        greet(jnp.where(y == 3, head + 7, head + 2 * y + 1))

    @pl.when(is_head)
    def _():
        greet(head + 1)
        for q in (1, 2, 3):
            greet(side * 8 + 2 * q)

    more = jnp.where(is_tail, 4, jnp.where(is_head, 0, 1))

    def remote(src, dst, send, recv, device):
        return pltpu.make_async_remote_copy(
            src_ref=src, dst_ref=dst, send_sem=send, recv_sem=recv, device_id=device, device_id_type=MESH
        )

    handoff = [
        remote(ids.at[0], pids, hs.at[0], hr.at[0], at(section=nxt)),
        remote(weights.at[0], pwts, hs.at[1], hr.at[1], at(section=nxt)),
    ]
    whole = remote(act, tok.at[1], hs.at[2], hr.at[2], at(section=nxt))

    def quarter(q):
        return pl.ds(q * 2 * CAP, 2 * CAP)

    parts = [
        remote(
            act.at[quarter(q)], relay, hs.at[3 + q], hr.at[3],
            at(section=side * 8 + 2 * q + 1 if q < 3 else head + 6),
        )
        for q in range(4)
    ]
    over = remote(relay, relay, hs.at[7], hr.at[3], at(section=head + 2 * y))
    over_last = remote(relay, tok.at[1, quarter(0)], hs.at[7], hr.at[4], at(section=head))
    home = [
        remote(relay, tok.at[1, quarter(q)], hs.at[7], hr.at[4 + q], at(section=side * 8))
        for q in range(1, 4)
    ]

    def handoff_start():
        @pl.when(is_tail)
        def _():
            for copy in parts:
                copy.start()

        @pl.when(jnp.logical_not(is_tail))
        def _():
            whole.start()

    def handoff_over():
        @pl.when(before)
        def _():
            over.wait_recv()

            @pl.when(y == 0)
            def _():
                over_last.start()

            @pl.when(y > 0)
            def _():
                over.start()

    def handoff_home():
        @pl.when(after)
        def _():
            over.wait_recv()
            for q in range(1, 4):

                @pl.when(y == q)
                def _():
                    home[q - 1].start()

    def handoff_arrived():
        @pl.when(is_head)
        def _():
            over_last.wait_recv()
            for copy in home:
                copy.wait_recv()

        @pl.when(jnp.logical_not(is_head))
        def _():
            whole.wait_recv()

    def handoff_sent():
        @pl.when(is_tail)
        def _():
            for copy in parts:
                copy.wait_send()

        @pl.when(jnp.logical_not(is_tail))
        def _():
            whole.wait_send()

        @pl.when(jnp.logical_or(before, after))
        def _():
            over.wait_send()
    experts = (p, lax.rem(p + dr + 4, 4), lax.rem(p - dr + 4, 4), lax.rem(p + 2, 4))
    sel[0] = routing(ids[0], weights[0], experts)[0]
    loads[0].wait()

    def prologue(r):
        total = jnp.zeros((4 * CAP, 128), F32)
        for n in range(0, width, 1024):
            cols = pl.ds(n, 1024)
            block = jnp.dot(sel[r], tok[2 * r, :, cols], preferred_element_type=F32)
            rows[:, cols] = block
            for m in range(0, 1024, 128):
                total += block[:, m : m + 128] * block[:, m : m + 128]
        scale = lax.rsqrt(jnp.sum(total, axis=1, keepdims=True) * (1.0 / width) + 1e-06)
        for n in range(0, width, 1024):
            cols = pl.ds(n, 1024)
            block = (rows[:, cols] * scale * gain[:, cols].astype(F32)).astype(BF16)
            own[r, unit(0), cols] = block[:CAP]
            for j in range(1, 4):
                sbuf[r, j, :, cols] = block[j * CAP : (j + 1) * CAP]

    def epilogue():
        for n in range(0, width, 1024):
            cols = pl.ds(n, 1024)
            tok[2, :, cols] = combine(coef[0], res[:, cols], tok[1, :, cols])

    def ffn(r, table, start, count, dst):
        chunk = pl.ds(start, count)

        @pl.loop(0, (2 * hidden) // 256)
        def _(n):
            cols = pl.ds(pl.multiple_of(n * 256, 256), 256)
            gu[pl.ds(0, count), cols] = jnp.dot(
                table[r, chunk, :], w1[:, cols], preferred_element_type=F32
            )

        gate, up = gu[pl.ds(0, count), pl.ds(0, hidden)], gu[pl.ds(0, count), pl.ds(hidden, hidden)]
        hid[pl.ds(0, count), :] = (gate / (1.0 + jnp.exp(-gate)) * up).astype(BF16)

        for n in range(0, width, 1024):
            cols = pl.ds(n, 1024)
            block = jnp.dot(hid[pl.ds(0, count), :], w2[:, cols], preferred_element_type=F32)
            if dst is pown:
                dst[chunk, cols] = block
            else:
                dst[r, chunk, cols] = block.astype(BF16)

    started = []
    for r in range(2):

        def channel(src, dst, index, device):
            copy = remote(src, dst, ssem.at[r, index], rsem.at[r, index], device)
            return copy

        up = {
            j: channel(sbuf.at[r, j], own.at[r, unit(j)], UP + j, at(d))
            for j, d in ((1, dr), (2, -2 * dr), (3, 3 * dr))
        }
        mate = {
            j: channel(own.at[r, unit(j)], own.at[r, unit(4 + j)], MATE + j, at(-dr))
            for j in range(4)
        }
        cross = {
            u: channel(own.at[r, unit(u)], par.at[r, unit(u)], CROSS + u, at(0, cross=True))
            for u in (0, 1, 2, 3, 5, 6, 7)
        }
        cross[4] = channel(par.at[r, unit(0)], par.at[r, unit(4)], CROSS + 4, at(-dr))
        back = {
            u: channel(psend.at[r, unit(u)], rx.at[r, unit(u)], BACK + u, at(0, cross=True))
            for u in (0, 1, 2, 3, 5, 6, 7)
        }
        back[4] = channel(psend.at[r, unit(4)], ppr.at[r], BACK + 4, at(-dr))
        pair = {
            j: channel(ms.at[r, j], rz.at[r, j], PAIR + j, at(-dr)) for j in range(4)
        }
        dest, target = (res, nxt) if r == 0 else (results, s)
        last = {
            j: channel(
                fs.at[r, j], dest.at[pl.ds(j * CAP, CAP)], LAST + j, at(dr * j, section=target)
            )
            for j in range(r, 4)
        }
        if r == 1:
            last[0] = pltpu.make_async_copy(
                fs.at[r, 0], results.at[pl.ds(0, CAP)], rsem.at[r, LAST]
            )

        def go(copy, tracked=True):
            copy.start()
            if tracked:
                started.append(copy)

        prologue(r)
        if r == 0:
            pl.semaphore_wait(barrier, len(near) + len(below) + more)
        go(cross[0])
        go(mate[0])
        go(up[1])
        go(up[3])
        go(up[2])
        if r == 0:
            for copy in handoff:
                copy.start()
            handoff_start()
            sel[1], coefs = routing(ids[1], weights[1], experts)
            coef[1] = split_coefs(coefs)
            keep_coefs.start()
            for load in loads[1:]:
                load.wait()
        mate[0].wait_recv()
        up[1].wait_recv()
        go(mate[1])
        go(cross[1])
        cross[0].wait_recv()
        go(cross[4])
        mate[1].wait_recv()
        go(cross[5])
        for j in (3, 2):
            up[j].wait_recv()
            go(mate[j])
            go(cross[j])
            mate[j].wait_recv()
            go(cross[4 + j])
        for u in (4, 1, 5):
            cross[u].wait_recv()
        ffn(r, par, 0, 4 * CAP, psend)
        go(back[5])
        go(back[1])
        go(back[4])
        if r == 0:
            handoff_over()
        ffn(r, own, 0, 8 * CAP, pown)
        ms[r, 0] = pown[unit(4), :].astype(BF16)
        go(pair[0])
        for u in (2, 6, 3, 7):
            cross[u].wait_recv()
        ffn(r, par, 4 * CAP, 4 * CAP, psend)
        for u in (7, 3, 6, 2):
            go(back[u])
        back[4].wait_recv()
        psend[r, unit(0), :] = (psend[r, unit(0), :].astype(F32) + ppr[r].astype(F32)).astype(BF16)
        go(back[0])
        if r == 0:
            handoff[0].wait_recv()
            handoff[1].wait_recv()
            coef[0] = split_coefs(routing(pids[...], pwts[...], experts)[1])

        def toward_mate(j):
            back[4 + j].wait_recv()
            ms[r, j] = (pown[unit(4 + j), :] + rx[r, unit(4 + j), :].astype(F32)).astype(BF16)
            go(pair[j])

        def finish(j):
            back[j].wait_recv()
            pair[j].wait_recv()
            fs[r, j] = (
                pown[unit(j), :] + rx[r, unit(j), :].astype(F32) + rz[r, j].astype(F32)
            ).astype(BF16)
            go(last[j], tracked=r == 0 or j > 0)

        toward_mate(1)
        toward_mate(3)
        finish(1)
        toward_mate(2)
        if r == 0:
            handoff_home()
        finish(3)

        finish(2)
        finish(0)
        if r == 0:
            for j in (1, 3, 2, 0):
                last[j].wait_recv()
            handoff_arrived()
            epilogue()
            keep_base.start()
        else:
            for j in (1, 3, 2):
                last[j].wait_recv()
            last[0].wait()

    keep_coefs.wait()
    keep_base.wait()
    for copy in started + handoff:
        copy.wait_send()
    handoff_sent()


def body(activations, norm_gain, w_gate, w_up, w_down, expert_ids, route_weights):
    tokens, width = activations.shape[1:]
    hidden = w_gate.shape[2]
    slots = 4 * CAP
    anywhere = pl.BlockSpec(memory_space=pl.ANY)
    vmem = pl.BlockSpec(memory_space=pltpu.VMEM)
    base, results, coefs = pl.pallas_call(
        kernel,
        out_shape=[
            jax.ShapeDtypeStruct((tokens, width), BF16),
            jax.ShapeDtypeStruct((slots, width), BF16),
            jax.ShapeDtypeStruct((tokens, 4 * slots), BF16),
        ],
        in_specs=[anywhere, vmem, anywhere, anywhere, anywhere, vmem, vmem],
        out_specs=[anywhere, anywhere, anywhere],
        scratch_shapes=[
            pltpu.VMEM((3, tokens, width), BF16),
            pltpu.VMEM((2, slots, tokens), BF16),
            pltpu.VMEM((2, tokens, 4 * slots), BF16),
            pltpu.VMEM((slots, width), F32),
            pltpu.VMEM((2, 4, CAP, width), BF16),
            pltpu.VMEM((2, 8 * CAP, width), BF16),
            pltpu.VMEM((2, 8 * CAP, width), BF16),
            pltpu.VMEM((8 * CAP, 2 * hidden), F32),
            pltpu.VMEM((8 * CAP, hidden), BF16),
            pltpu.VMEM((2, 8 * CAP, width), BF16),
            pltpu.VMEM((8 * CAP, width), F32),
            pltpu.VMEM((2, 8 * CAP, width), BF16),
            pltpu.VMEM((2, 4, CAP, width), BF16),
            pltpu.VMEM((2, 4, CAP, width), BF16),
            pltpu.VMEM((2, 4, CAP, width), BF16),
            pltpu.VMEM((slots, width), BF16),
            pltpu.VMEM((width, 2 * hidden), BF16),
            pltpu.VMEM((hidden, width), BF16),
            pltpu.VMEM((8, tokens), jnp.int32),
            pltpu.VMEM((8, tokens), F32),
            pltpu.VMEM((2 * CAP, width), BF16),
            pltpu.VMEM((2, CAP, width), BF16),
            pltpu.SemaphoreType.DMA((2, CHANNELS)),
            pltpu.SemaphoreType.DMA((2, CHANNELS)),
            pltpu.SemaphoreType.DMA((8,)),
            pltpu.SemaphoreType.DMA((8,)),
            pltpu.SemaphoreType.DMA((6,)),
        ],
        compiler_params=pltpu.CompilerParams(
            collective_id=0, has_side_effects=True, vmem_limit_bytes=56 << 20
        ),
        cost_estimate=pl.CostEstimate(
            flops=12 * 256 * width * hidden, bytes_accessed=12 << 20, transcendentals=512 * hidden
        ),
    )(
        activations[0],
        norm_gain,
        w_gate[0],
        w_up[0],
        w_down[0],
        jnp.swapaxes(expert_ids[:, 0], 1, 2),
        jnp.swapaxes(route_weights[:, 0], 1, 2),
    )
    step = 1024
    pieces = width // step
    return pl.pallas_call(
        last_step,
        out_shape=jax.ShapeDtypeStruct((1, tokens, width), BF16),
        in_specs=[anywhere] * 3,
        out_specs=anywhere,
        scratch_shapes=[
            pltpu.VMEM((tokens, 4 * slots), BF16),
            pltpu.VMEM((pieces, slots, step), BF16),
            pltpu.VMEM((pieces, tokens, step), BF16),
            pltpu.VMEM((pieces, tokens, step), BF16),
            pltpu.SemaphoreType.DMA((2 * pieces + 1,)),
            pltpu.SemaphoreType.DMA((pieces,)),
        ],
        compiler_params=pltpu.CompilerParams(vmem_limit_bytes=56 << 20),
    )(coefs, results, base)


def solution(mesh):
    return jax.shard_map(
        body,
        mesh=mesh,
        in_specs=(
            P("section", "expert", None),
            P("section", None),
            P("section", None, "expert"),
            P("section", None, "expert"),
            P("section", "expert", None),
            P(None, "section", "expert", None),
            P(None, "section", "expert", None),
        ),
        out_specs=P("section", "expert", None),
        check_vma=False,
    )
```

```python
import functools

import jax
import jax.numpy as jnp
from jax import lax
from jax.experimental import pallas as pl
from jax.experimental.pallas import tpu as pltpu
from jax.sharding import PartitionSpec as P

MESH = pl.DeviceIdType.MESH
F32, BF16 = jnp.float32, jnp.bfloat16
POS = {0: 0, 4: 1, 1: 2, 5: 3, 2: 4, 6: 5, 3: 6, 7: 7}
CAP = 16
UP, MATE, CROSS, BACK, PAIR, LAST = 0, 4, 8, 16, 24, 28
CHANNELS = 32
PIECES = 2
BEHIND = 3


def unit(u):
    return pl.ds(POS[u] * CAP, CAP)


def routing(ids, weights, experts):
    tokens = ids.shape[1]
    matched, factors = [], []
    for e in experts:
        hit = ids == e
        matched.append(jnp.max(jnp.where(hit, 1.0, 0.0), axis=0, keepdims=True))
        factors.append(jnp.sum(jnp.where(hit, weights, 0.0), axis=0, keepdims=True))
    named = jnp.concatenate(matched + matched, axis=0)
    earlier = lax.broadcasted_iota(jnp.int32, (tokens, tokens), 0) < lax.broadcasted_iota(
        jnp.int32, (tokens, tokens), 1
    )
    rank = jnp.dot(
        named.astype(BF16), jnp.where(earlier, 1.0, 0.0).astype(BF16), preferred_element_type=F32
    )
    slot = lax.broadcasted_iota(jnp.int32, (CAP, tokens), 0).astype(F32)
    select = [
        jnp.where(jnp.logical_and(rank[j : j + 1] == slot, matched[j] > 0.5), 1.0, 0.0)
        for j in range(4)
    ]
    coefs = jnp.concatenate([select[j] * factors[j] for j in range(4)], axis=0)
    return jnp.concatenate(select, axis=0).astype(BF16), coefs


def split_coefs(coefs):
    first = coefs.astype(BF16).astype(F32)
    second = (coefs - first).astype(BF16).astype(F32)
    third = coefs - first - second
    left = jnp.concatenate([first, second], axis=0).T
    right = jnp.concatenate([third, jnp.zeros_like(third)], axis=0).T
    return jnp.concatenate([left, right], axis=1).astype(BF16)


def combine(coefs, results, carried):
    mixed = jnp.dot(coefs, jnp.concatenate([results] * 4, axis=0), preferred_element_type=F32)
    return (carried.astype(F32) + mixed).astype(BF16)


def last_step(coefs, results, carried, out, c, r, t, o, sems, osems):
    step = r.shape[2]
    loads = [pltpu.make_async_copy(coefs, c, sems.at[0])]
    for n in range(r.shape[0]):
        cols = pl.ds(n * step, step)
        loads.append(pltpu.make_async_copy(results.at[:, cols], r.at[n], sems.at[2 * n + 1]))
        loads.append(pltpu.make_async_copy(carried.at[:, cols], t.at[n], sems.at[2 * n + 2]))
    for load in loads:
        load.start()
    loads[0].wait()
    stores = []
    for n in range(r.shape[0]):
        loads[2 * n + 1].wait()
        loads[2 * n + 2].wait()
        o[n] = combine(c[...], r[n], t[n])
        stores.append(pltpu.make_async_copy(o.at[n], out.at[0, :, pl.ds(n * step, step)], osems.at[n]))
        stores[n].start()
    for store in stores:
        store.wait()


def kernel(
    act, gain, wg, wu, wd, ids, weights, base, results, coefs1,
    tok, sel, coef, rows, sbuf, own, par, gu, hid, psend, pown, rx, ms, rz, fs, res, w1, w2, pids, pwts,
    relay, ppr, ssem, rsem, hs, hr, lsem,
):
    s, k = lax.axis_index("section"), lax.axis_index("expert")
    sections = lax.axis_size("section")
    z, h = k // 2, lax.rem(k, 2)
    b = lax.rem(z, 2)
    dr = 2 * b - 1
    p = z // 2
    width = tok.shape[2]
    hidden = wd.shape[0]
    nxt, prv = lax.rem(s + 1, sections), lax.rem(s + sections - 1, sections)

    def at(dz=0, cross=False, section=None):
        there = lax.rem(z + dz + 8, 8) * 2 + (1 - h if cross else h)
        return (s if section is None else section, there)

    loads = [
        pltpu.make_async_copy(act, tok.at[0], lsem.at[0]),
        pltpu.make_async_copy(wg, w1.at[:, pl.ds(0, hidden)], lsem.at[1]),
        pltpu.make_async_copy(wu, w1.at[:, pl.ds(hidden, hidden)], lsem.at[2]),
        pltpu.make_async_copy(wd, w2, lsem.at[3]),
    ]
    for load in loads:
        load.start()
    keep_coefs = pltpu.make_async_copy(coef.at[1], coefs1, lsem.at[4])
    keep_base = pltpu.make_async_copy(tok.at[2], base, lsem.at[5])

    barrier = pltpu.get_barrier_semaphore()
    near = [at(dr), at(2 * dr), at(-2 * dr), at(3 * dr), at(-dr), at(0, cross=True)]
    below = [at(j, section=prv) for j in (0, dr, -2 * dr, 3 * dr)]
    for device in near + below:
        pl.semaphore_signal(barrier, inc=1, device_id=device, device_id_type=MESH)

    side, y, core = s // 8, lax.rem(s // 2, 4), lax.rem(s, 2)
    tail, head = side * 8 + 7, (1 - side) * 8
    is_tail = jnp.logical_and(y == 3, core == 1)
    is_head = jnp.logical_and(y == 0, core == 0)
    before = jnp.logical_and(y < 3, core == 1)
    after = jnp.logical_and(y > 0, core == 0)

    def greet(section):
        pl.semaphore_signal(barrier, inc=1, device_id=at(section=section), device_id_type=MESH)

    @pl.when(before)
    def _():
        greet(tail)

    @pl.when(after)
    def _():
        greet(jnp.where(y == 3, head + 7, head + 2 * y + 1))

    @pl.when(is_head)
    def _():
        greet(head + 1)
        for q in (1, 2, 3):
            greet(side * 8 + 2 * q)

    more = jnp.where(is_tail, 4, jnp.where(is_head, 0, 1))

    def remote(src, dst, send, recv, device):
        return pltpu.make_async_remote_copy(
            src_ref=src, dst_ref=dst, send_sem=send, recv_sem=recv, device_id=device, device_id_type=MESH
        )

    handoff = [
        remote(ids.at[0], pids, hs.at[0], hr.at[0], at(section=nxt)),
        remote(weights.at[0], pwts, hs.at[1], hr.at[1], at(section=nxt)),
    ]
    whole = remote(act, tok.at[1], hs.at[2], hr.at[2], at(section=nxt))

    def quarter(q):
        return pl.ds(q * 2 * CAP, 2 * CAP)

    parts = [
        remote(
            act.at[quarter(q)], relay, hs.at[3 + q], hr.at[3],
            at(section=side * 8 + 2 * q + 1 if q < 3 else head + 6),
        )
        for q in range(4)
    ]
    over = remote(relay, relay, hs.at[7], hr.at[3], at(section=head + 2 * y))
    over_last = remote(relay, tok.at[1, quarter(0)], hs.at[7], hr.at[4], at(section=head))
    home = [
        remote(relay, tok.at[1, quarter(q)], hs.at[7], hr.at[4 + q], at(section=side * 8))
        for q in range(1, 4)
    ]

    def handoff_start():
        @pl.when(is_tail)
        def _():
            for copy in parts:
                copy.start()

        @pl.when(jnp.logical_not(is_tail))
        def _():
            whole.start()

    def handoff_over():
        @pl.when(before)
        def _():
            over.wait_recv()

            @pl.when(y == 0)
            def _():
                over_last.start()

            @pl.when(y > 0)
            def _():
                over.start()

    def handoff_home():
        @pl.when(after)
        def _():
            over.wait_recv()
            for q in range(1, 4):

                @pl.when(y == q)
                def _():
                    home[q - 1].start()

    def handoff_arrived():
        @pl.when(is_head)
        def _():
            over_last.wait_recv()
            for copy in home:
                copy.wait_recv()

        @pl.when(jnp.logical_not(is_head))
        def _():
            whole.wait_recv()

    def handoff_sent():
        @pl.when(is_tail)
        def _():
            for copy in parts:
                copy.wait_send()

        @pl.when(jnp.logical_not(is_tail))
        def _():
            whole.wait_send()

        @pl.when(jnp.logical_or(before, after))
        def _():
            over.wait_send()
    experts = (p, lax.rem(p + dr + 4, 4), lax.rem(p - dr + 4, 4), lax.rem(p + 2, 4))
    sel[0] = routing(ids[0], weights[0], experts)[0]
    loads[0].wait()

    def prologue(r):
        total = jnp.zeros((4 * CAP, 128), F32)
        for n in range(0, width, 1024):
            cols = pl.ds(n, 1024)
            block = jnp.dot(sel[r], tok[2 * r, :, cols], preferred_element_type=F32)
            rows[:, cols] = block
            for m in range(0, 1024, 128):
                total += block[:, m : m + 128] * block[:, m : m + 128]
        scale = lax.rsqrt(jnp.sum(total, axis=1, keepdims=True) * (1.0 / width) + 1e-06)
        for n in range(0, width, 1024):
            cols = pl.ds(n, 1024)
            block = (rows[:, cols] * scale * gain[:, cols].astype(F32)).astype(BF16)
            own[r, unit(0), cols] = block[:CAP]
            for j in range(1, 4):
                sbuf[r, j, :, cols] = block[j * CAP : (j + 1) * CAP]

    def epilogue():
        for n in range(0, width, 1024):
            cols = pl.ds(n, 1024)
            tok[2, :, cols] = combine(coef[0], res[:, cols], tok[1, :, cols])

    def ffn(r, table, start, count, dst):
        chunk = pl.ds(start, count)

        @pl.loop(0, (2 * hidden) // 256)
        def _(n):
            cols = pl.ds(pl.multiple_of(n * 256, 256), 256)
            gu[pl.ds(0, count), cols] = jnp.dot(
                table[r, chunk, :], w1[:, cols], preferred_element_type=F32
            )

        gate, up = gu[pl.ds(0, count), pl.ds(0, hidden)], gu[pl.ds(0, count), pl.ds(hidden, hidden)]
        hid[pl.ds(0, count), :] = (gate / (1.0 + jnp.exp(-gate)) * up).astype(BF16)

        for n in range(0, width, 1024):
            cols = pl.ds(n, 1024)
            block = jnp.dot(hid[pl.ds(0, count), :], w2[:, cols], preferred_element_type=F32)
            if dst is pown:
                dst[chunk, cols] = block
            else:
                dst[r, chunk, cols] = block.astype(BF16)

    started = []

    def piece(q):
        return pl.ds(q * (width // PIECES), width // PIECES)

    for r in range(2):

        def channel(src, dst, index, device):
            return [
                remote(
                    src.at[:, piece(q)], dst.at[:, piece(q)],
                    ssem.at[r, index * PIECES + q], rsem.at[r, index * PIECES + q], device,
                )
                for q in range(PIECES)
            ]

        up = {
            j: channel(sbuf.at[r, j], own.at[r, unit(j)], UP + j, at(d))
            for j, d in ((1, dr), (2, -2 * dr), (3, 3 * dr))
        }
        mate = {
            j: channel(own.at[r, unit(j)], own.at[r, unit(4 + j)], MATE + j, at(-dr))
            for j in range(4)
        }
        cross = {
            u: channel(own.at[r, unit(u)], par.at[r, unit(u)], CROSS + u, at(0, cross=True))
            for u in (0, 1, 2, 3, 5, 6, 7)
        }
        cross[4] = channel(par.at[r, unit(0)], par.at[r, unit(4)], CROSS + 4, at(-dr))
        back = {
            u: channel(psend.at[r, unit(u)], rx.at[r, unit(u)], BACK + u, at(0, cross=True))
            for u in (0, 1, 2, 3, 5, 6, 7)
        }
        back[4] = channel(psend.at[r, unit(4)], ppr.at[r], BACK + 4, at(-dr))
        pair = {
            j: channel(ms.at[r, j], rz.at[r, j], PAIR + j, at(-dr)) for j in range(4)
        }
        dest, target = (res, nxt) if r == 0 else (results, s)
        last = {
            j: channel(
                fs.at[r, j], dest.at[pl.ds(j * CAP, CAP)], LAST + j, at(dr * j, section=target)
            )
            for j in range(r, 4)
        }
        if r == 1:
            last[0] = [
                pltpu.make_async_copy(
                    fs.at[r, 0, :, piece(q)],
                    results.at[pl.ds(0, CAP), piece(q)],
                    rsem.at[r, LAST * PIECES + q],
                )
                for q in range(PIECES)
            ]

        def go(copies, tracked=True):
            for copy in copies:
                copy.start()
                if tracked:
                    started.append(copy)

        def arrived(copies):
            for copy in copies:
                copy.wait_recv()

        prologue(r)
        if r == 0:
            pl.semaphore_wait(barrier, len(near) + len(below) + more)
        for q in range(PIECES):
            go(cross[0][q : q + 1])
            go(mate[0][q : q + 1])
        for j in (1,2,3):
            go(up[j])
        if r == 0:
            for copy in handoff:
                copy.start()
            handoff_start()
            sel[1], coefs = routing(ids[1], weights[1], experts)
            coef[1] = split_coefs(coefs)
            keep_coefs.start()
            for load in loads[1:]:
                load.wait()
        behind = []

        def forward(j, q):
            arrived(mate[j][q : q + 1])
            go(cross[4 + j][q : q + 1])

        for n, j in enumerate((1,2,3)):
            for q in range(PIECES):
                arrived(up[j][q : q + 1])
                go(mate[j][q : q + 1])
                go(cross[j][q : q + 1])
                behind.append((j, q))
                if len(behind) > BEHIND:
                    forward(*behind.pop(0))
            if n == 0:
                arrived(mate[0])
                arrived(cross[0])
                go(cross[4])
        for j, q in behind:
            forward(j, q)
        for u in (4, 1, 5):
            arrived(cross[u])
        ffn(r, par, 0, 4 * CAP, psend)
        go(back[5])
        go(back[1])
        go(back[4])
        if r == 0:
            handoff_over()
        ffn(r, own, 0, 8 * CAP, pown)
        ms[r, 0] = pown[unit(4), :].astype(BF16)
        go(pair[0])
        for u in (2, 6, 3, 7):
            arrived(cross[u])
        ffn(r, par, 4 * CAP, 4 * CAP, psend)
        for u in (7, 3, 6, 2):
            go(back[u])
        arrived(back[4])
        psend[r, unit(0), :] = (psend[r, unit(0), :].astype(F32) + ppr[r].astype(F32)).astype(BF16)
        go(back[0])
        if r == 0:
            handoff[0].wait_recv()
            handoff[1].wait_recv()
            coef[0] = split_coefs(routing(pids[...], pwts[...], experts)[1])

        def toward_mate(j):
            for q in range(PIECES):
                arrived(back[4 + j][q : q + 1])
                mine, got = pown[unit(4 + j), piece(q)], rx[r, unit(4 + j), piece(q)]
                ms[r, j, :, piece(q)] = (mine + got.astype(F32)).astype(BF16)
                go(pair[j][q : q + 1])

        def finish(j):
            for q in range(PIECES):
                arrived(back[j][q : q + 1])
                arrived(pair[j][q : q + 1])
                mine, got = pown[unit(j), piece(q)], rx[r, unit(j), piece(q)]
                summed = mine + got.astype(F32) + rz[r, j, :, piece(q)].astype(F32)
                fs[r, j, :, piece(q)] = summed.astype(BF16)
                go(last[j][q : q + 1], tracked=r == 0 or j > 0)

        toward_mate(1)
        toward_mate(3)
        finish(1)
        toward_mate(2)
        if r == 0:
            handoff_home()
        finish(3)

        finish(2)
        finish(0)
        if r == 0:
            for j in (1, 3, 2, 0):
                arrived(last[j])
            handoff_arrived()
            epilogue()
            keep_base.start()
        else:
            for j in (1, 3, 2):
                arrived(last[j])
            for copy in last[0]:
                copy.wait()

    keep_coefs.wait()
    keep_base.wait()
    for copy in started + handoff:
        copy.wait_send()
    handoff_sent()


def body(activations, norm_gain, w_gate, w_up, w_down, expert_ids, route_weights):
    tokens, width = activations.shape[1:]
    hidden = w_gate.shape[2]
    slots = 4 * CAP
    anywhere = pl.BlockSpec(memory_space=pl.ANY)
    vmem = pl.BlockSpec(memory_space=pltpu.VMEM)
    base, results, coefs = pl.pallas_call(
        kernel,
        out_shape=[
            jax.ShapeDtypeStruct((tokens, width), BF16),
            jax.ShapeDtypeStruct((slots, width), BF16),
            jax.ShapeDtypeStruct((tokens, 4 * slots), BF16),
        ],
        in_specs=[anywhere, vmem, anywhere, anywhere, anywhere, vmem, vmem],
        out_specs=[anywhere, anywhere, anywhere],
        scratch_shapes=[
            pltpu.VMEM((3, tokens, width), BF16),
            pltpu.VMEM((2, slots, tokens), BF16),
            pltpu.VMEM((2, tokens, 4 * slots), BF16),
            pltpu.VMEM((slots, width), F32),
            pltpu.VMEM((2, 4, CAP, width), BF16),
            pltpu.VMEM((2, 8 * CAP, width), BF16),
            pltpu.VMEM((2, 8 * CAP, width), BF16),
            pltpu.VMEM((8 * CAP, 2 * hidden), F32),
            pltpu.VMEM((8 * CAP, hidden), BF16),
            pltpu.VMEM((2, 8 * CAP, width), BF16),
            pltpu.VMEM((8 * CAP, width), F32),
            pltpu.VMEM((2, 8 * CAP, width), BF16),
            pltpu.VMEM((2, 4, CAP, width), BF16),
            pltpu.VMEM((2, 4, CAP, width), BF16),
            pltpu.VMEM((2, 4, CAP, width), BF16),
            pltpu.VMEM((slots, width), BF16),
            pltpu.VMEM((width, 2 * hidden), BF16),
            pltpu.VMEM((hidden, width), BF16),
            pltpu.VMEM((8, tokens), jnp.int32),
            pltpu.VMEM((8, tokens), F32),
            pltpu.VMEM((2 * CAP, width), BF16),
            pltpu.VMEM((2, CAP, width), BF16),
            pltpu.SemaphoreType.DMA((2, CHANNELS * PIECES)),
            pltpu.SemaphoreType.DMA((2, CHANNELS * PIECES)),
            pltpu.SemaphoreType.DMA((8,)),
            pltpu.SemaphoreType.DMA((8,)),
            pltpu.SemaphoreType.DMA((6,)),
        ],
        compiler_params=pltpu.CompilerParams(
            collective_id=0, has_side_effects=True, vmem_limit_bytes=56 << 20
        ),
        cost_estimate=pl.CostEstimate(
            flops=12 * 256 * width * hidden, bytes_accessed=12 << 20, transcendentals=512 * hidden
        ),
    )(
        activations[0],
        norm_gain,
        w_gate[0],
        w_up[0],
        w_down[0],
        jnp.swapaxes(expert_ids[:, 0], 1, 2),
        jnp.swapaxes(route_weights[:, 0], 1, 2),
    )
    step = 1024
    pieces = width // step
    return pl.pallas_call(
        last_step,
        out_shape=jax.ShapeDtypeStruct((1, tokens, width), BF16),
        in_specs=[anywhere] * 3,
        out_specs=anywhere,
        scratch_shapes=[
            pltpu.VMEM((tokens, 4 * slots), BF16),
            pltpu.VMEM((pieces, slots, step), BF16),
            pltpu.VMEM((pieces, tokens, step), BF16),
            pltpu.VMEM((pieces, tokens, step), BF16),
            pltpu.SemaphoreType.DMA((2 * pieces + 1,)),
            pltpu.SemaphoreType.DMA((pieces,)),
        ],
        compiler_params=pltpu.CompilerParams(vmem_limit_bytes=56 << 20),
    )(coefs, results, base)


def solution(mesh):
    return jax.shard_map(
        body,
        mesh=mesh,
        in_specs=(
            P("section", "expert", None),
            P("section", None),
            P("section", None, "expert"),
            P("section", None, "expert"),
            P("section", "expert", None),
            P(None, "section", "expert", None),
            P(None, "section", "expert", None),
        ),
        out_specs=P("section", "expert", None),
        check_vma=False,
    )
```

```python
import functools

import jax
import jax.numpy as jnp
from jax import lax
from jax.experimental import pallas as pl
from jax.experimental.pallas import tpu as pltpu
from jax.sharding import PartitionSpec as P

MESH = pl.DeviceIdType.MESH
F32, BF16 = jnp.float32, jnp.bfloat16
POS = {0: 0, 4: 1, 1: 2, 5: 3, 2: 4, 6: 5, 3: 6, 7: 7}
CAP = 16
UP, MATE, CROSS, BACK, PAIR, LAST = 0, 4, 8, 16, 24, 28
CHANNELS = 32
PIECES = 2
SHARED = 2
BEHIND = 3


def unit(u):
    return pl.ds(POS[u] * CAP, CAP)


def routing(ids, weights, experts):
    tokens = ids.shape[1]
    matched, factors = [], []
    for e in experts:
        hit = ids == e
        matched.append(jnp.max(jnp.where(hit, 1.0, 0.0), axis=0, keepdims=True))
        factors.append(jnp.sum(jnp.where(hit, weights, 0.0), axis=0, keepdims=True))
    named = jnp.concatenate(matched + matched, axis=0)
    earlier = lax.broadcasted_iota(jnp.int32, (tokens, tokens), 0) < lax.broadcasted_iota(
        jnp.int32, (tokens, tokens), 1
    )
    rank = jnp.dot(
        named.astype(BF16), jnp.where(earlier, 1.0, 0.0).astype(BF16), preferred_element_type=F32
    )
    slot = lax.broadcasted_iota(jnp.int32, (CAP, tokens), 0).astype(F32)
    select = [
        jnp.where(jnp.logical_and(rank[j : j + 1] == slot, matched[j] > 0.5), 1.0, 0.0)
        for j in range(4)
    ]
    coefs = jnp.concatenate([select[j] * factors[j] for j in range(4)], axis=0)
    return jnp.concatenate(select, axis=0).astype(BF16), coefs


def split_coefs(coefs):
    first = coefs.astype(BF16).astype(F32)
    second = (coefs - first).astype(BF16).astype(F32)
    third = coefs - first - second
    left = jnp.concatenate([first, second], axis=0).T
    right = jnp.concatenate([third, jnp.zeros_like(third)], axis=0).T
    return jnp.concatenate([left, right], axis=1).astype(BF16)


def combine(coefs, results, carried):
    mixed = jnp.dot(coefs, jnp.concatenate([results] * 4, axis=0), preferred_element_type=F32)
    return (carried.astype(F32) + mixed).astype(BF16)


def last_step(coefs, results, carried, out, c, r, t, o, sems, osems):
    step = r.shape[2]
    loads = [pltpu.make_async_copy(coefs, c, sems.at[0])]
    for n in range(r.shape[0]):
        cols = pl.ds(n * step, step)
        loads.append(pltpu.make_async_copy(results.at[:, cols], r.at[n], sems.at[2 * n + 1]))
        loads.append(pltpu.make_async_copy(carried.at[:, cols], t.at[n], sems.at[2 * n + 2]))
    for load in loads:
        load.start()
    loads[0].wait()
    stores = []
    for n in range(r.shape[0]):
        loads[2 * n + 1].wait()
        loads[2 * n + 2].wait()
        o[n] = combine(c[...], r[n], t[n])
        stores.append(pltpu.make_async_copy(o.at[n], out.at[0, :, pl.ds(n * step, step)], osems.at[n]))
        stores[n].start()
    for store in stores:
        store.wait()


def kernel(
    act, gain, wg, wu, wd, ids, weights, base, results, coefs1,
    tok, sel, coef, rows, sbuf, own, par, gu, hid, psend, pown, rx, ms, rz, fs, res, w1, w2, pids, pwts,
    relay, ppr, ssem, rsem, hs, hr, lsem,
):
    s, k = lax.axis_index("section"), lax.axis_index("expert")
    sections = lax.axis_size("section")
    z, h = k // 2, lax.rem(k, 2)
    b = lax.rem(z, 2)
    dr = 2 * b - 1
    p = z // 2
    width = tok.shape[2]
    hidden = wd.shape[0]
    nxt, prv = lax.rem(s + 1, sections), lax.rem(s + sections - 1, sections)

    def at(dz=0, cross=False, section=None):
        there = lax.rem(z + dz + 8, 8) * 2 + (1 - h if cross else h)
        return (s if section is None else section, there)

    loads = [
        pltpu.make_async_copy(act, tok.at[0], lsem.at[0]),
        pltpu.make_async_copy(wg, w1.at[:, pl.ds(0, hidden)], lsem.at[1]),
        pltpu.make_async_copy(wu, w1.at[:, pl.ds(hidden, hidden)], lsem.at[2]),
        pltpu.make_async_copy(wd, w2, lsem.at[3]),
    ]
    for load in loads:
        load.start()
    keep_coefs = pltpu.make_async_copy(coef.at[1], coefs1, lsem.at[4])
    keep_base = pltpu.make_async_copy(tok.at[2], base, lsem.at[5])

    barrier = pltpu.get_barrier_semaphore()
    near = [at(dr), at(2 * dr), at(-2 * dr), at(3 * dr), at(-dr), at(0, cross=True)]
    below = [at(j, section=prv) for j in (0, dr, -2 * dr, 3 * dr)]
    for device in near + below:
        pl.semaphore_signal(barrier, inc=1, device_id=device, device_id_type=MESH)

    side, y, core = s // 8, lax.rem(s // 2, 4), lax.rem(s, 2)
    tail, head = side * 8 + 7, (1 - side) * 8
    is_tail = jnp.logical_and(y == 3, core == 1)
    is_head = jnp.logical_and(y == 0, core == 0)
    before = jnp.logical_and(y < 3, core == 1)
    after = jnp.logical_and(y > 0, core == 0)

    def greet(section):
        pl.semaphore_signal(barrier, inc=1, device_id=at(section=section), device_id_type=MESH)

    @pl.when(before)
    def _():
        greet(tail)

    @pl.when(after)
    def _():
        greet(jnp.where(y == 3, head + 7, head + 2 * y + 1))

    @pl.when(is_head)
    def _():
        greet(head + 1)
        for q in (1, 2, 3):
            greet(side * 8 + 2 * q)

    more = jnp.where(is_tail, 4, jnp.where(is_head, 0, 1))

    def remote(src, dst, send, recv, device):
        return pltpu.make_async_remote_copy(
            src_ref=src, dst_ref=dst, send_sem=send, recv_sem=recv, device_id=device, device_id_type=MESH
        )

    handoff = [
        remote(ids.at[0], pids, hs.at[0], hr.at[0], at(section=nxt)),
        remote(weights.at[0], pwts, hs.at[1], hr.at[1], at(section=nxt)),
    ]
    whole = remote(act, tok.at[1], hs.at[2], hr.at[2], at(section=nxt))

    def quarter(q):
        return pl.ds(q * 2 * CAP, 2 * CAP)

    parts = [
        remote(
            act.at[quarter(q)], relay, hs.at[3 + q], hr.at[3],
            at(section=side * 8 + 2 * q + 1 if q < 3 else head + 6),
        )
        for q in range(4)
    ]
    over = remote(relay, relay, hs.at[7], hr.at[3], at(section=head + 2 * y))
    over_last = remote(relay, tok.at[1, quarter(0)], hs.at[7], hr.at[4], at(section=head))
    home = [
        remote(relay, tok.at[1, quarter(q)], hs.at[7], hr.at[4 + q], at(section=side * 8))
        for q in range(1, 4)
    ]

    def handoff_start():
        @pl.when(is_tail)
        def _():
            for copy in parts:
                copy.start()

        @pl.when(jnp.logical_not(is_tail))
        def _():
            whole.start()

    def handoff_over():
        @pl.when(before)
        def _():
            over.wait_recv()

            @pl.when(y == 0)
            def _():
                over_last.start()

            @pl.when(y > 0)
            def _():
                over.start()

    def handoff_home():
        @pl.when(after)
        def _():
            over.wait_recv()
            for q in range(1, 4):

                @pl.when(y == q)
                def _():
                    home[q - 1].start()

    def handoff_arrived():
        @pl.when(is_head)
        def _():
            over_last.wait_recv()
            for copy in home:
                copy.wait_recv()

        @pl.when(jnp.logical_not(is_head))
        def _():
            whole.wait_recv()

    def handoff_sent():
        @pl.when(is_tail)
        def _():
            for copy in parts:
                copy.wait_send()

        @pl.when(jnp.logical_not(is_tail))
        def _():
            whole.wait_send()

        @pl.when(jnp.logical_or(before, after))
        def _():
            over.wait_send()
    experts = (p, lax.rem(p + dr + 4, 4), lax.rem(p - dr + 4, 4), lax.rem(p + 2, 4))
    sel[0] = routing(ids[0], weights[0], experts)[0]
    loads[0].wait()

    def prologue(r):
        total = jnp.zeros((4 * CAP, 128), F32)
        for n in range(0, width, 1024):
            cols = pl.ds(n, 1024)
            block = jnp.dot(sel[r], tok[2 * r, :, cols], preferred_element_type=F32)
            rows[:, cols] = block
            for m in range(0, 1024, 128):
                total += block[:, m : m + 128] * block[:, m : m + 128]
        scale = lax.rsqrt(jnp.sum(total, axis=1, keepdims=True) * (1.0 / width) + 1e-06)
        for n in range(0, width, 1024):
            cols = pl.ds(n, 1024)
            block = (rows[:, cols] * scale * gain[:, cols].astype(F32)).astype(BF16)
            own[r, unit(0), cols] = block[:CAP]
            for j in range(1, 4):
                sbuf[r, j, :, cols] = block[j * CAP : (j + 1) * CAP]

    def epilogue():
        for n in range(0, width, 1024):
            cols = pl.ds(n, 1024)
            tok[2, :, cols] = combine(coef[0], res[:, cols], tok[1, :, cols])

    def ffn(r, table, start, count, dst):
        chunk = pl.ds(start, count)

        @pl.loop(0, (2 * hidden) // 256)
        def _(n):
            cols = pl.ds(pl.multiple_of(n * 256, 256), 256)
            gu[pl.ds(0, count), cols] = jnp.dot(
                table[r, chunk, :], w1[:, cols], preferred_element_type=F32
            )

        gate, up = gu[pl.ds(0, count), pl.ds(0, hidden)], gu[pl.ds(0, count), pl.ds(hidden, hidden)]
        hid[pl.ds(0, count), :] = (gate / (1.0 + jnp.exp(-gate)) * up).astype(BF16)

        for n in range(0, width, 1024):
            cols = pl.ds(n, 1024)
            block = jnp.dot(hid[pl.ds(0, count), :], w2[:, cols], preferred_element_type=F32)
            if dst is pown:
                dst[chunk, cols] = block
            else:
                dst[r, chunk, cols] = block.astype(BF16)

    started = []

    def piece(q):
        return pl.ds(q * (width // PIECES), width // PIECES)

    for r in range(2):

        def channel(src, dst, index, device):
            return [
                remote(
                    src.at[:, piece(q)], dst.at[:, piece(q)],
                    ssem.at[r, index * PIECES + q], rsem.at[r, index * PIECES + q], device,
                )
                for q in range(PIECES)
            ]

        up = {
            j: channel(sbuf.at[r, j], own.at[r, unit(j)], UP + j, at(d))
            for j, d in ((1, dr), (2, -2 * dr), (3, 3 * dr))
        }
        mate = {
            j: channel(own.at[r, unit(j)], own.at[r, unit(4 + j)], MATE + j, at(-dr))
            for j in range(4)
        }
        cross = {
            u: channel(own.at[r, unit(u)], par.at[r, unit(u)], CROSS + u, at(0, cross=True))
            for u in range(8)
            if u != 4 + SHARED
        }
        cross[4 + SHARED] = channel(
            par.at[r, unit(SHARED)], par.at[r, unit(4 + SHARED)], CROSS + 4 + SHARED, at(-dr)
        )
        back = {
            u: channel(psend.at[r, unit(u)], rx.at[r, unit(u)], BACK + u, at(0, cross=True))
            for u in (0, 1, 2, 3, 5, 6, 7)
        }
        back[4] = channel(psend.at[r, unit(4)], ppr.at[r], BACK + 4, at(-dr))
        pair = {
            j: channel(ms.at[r, j], rz.at[r, j], PAIR + j, at(-dr)) for j in range(4)
        }
        dest, target = (res, nxt) if r == 0 else (results, s)
        last = {
            j: channel(
                fs.at[r, j], dest.at[pl.ds(j * CAP, CAP)], LAST + j, at(dr * j, section=target)
            )
            for j in range(r, 4)
        }
        if r == 1:
            last[0] = [
                pltpu.make_async_copy(
                    fs.at[r, 0, :, piece(q)],
                    results.at[pl.ds(0, CAP), piece(q)],
                    rsem.at[r, LAST * PIECES + q],
                )
                for q in range(PIECES)
            ]

        def go(copies, tracked=True):
            for copy in copies:
                copy.start()
                if tracked:
                    started.append(copy)

        def arrived(copies):
            for copy in copies:
                copy.wait_recv()

        prologue(r)
        if r == 0:
            pl.semaphore_wait(barrier, len(near) + len(below) + more)
        for q in range(PIECES):
            go(cross[0][q : q + 1])
            go(mate[0][q : q + 1])
        for j in (1, 2, 3):
            go(up[j])
        if r == 0:
            for copy in handoff:
                copy.start()
            handoff_start()
            sel[1], coefs = routing(ids[1], weights[1], experts)
            coef[1] = split_coefs(coefs)
            keep_coefs.start()
            for load in loads[1:]:
                load.wait()
        behind = []

        def forward(j, q):
            arrived(mate[j][q : q + 1])
            if j != SHARED:
                go(cross[4 + j][q : q + 1])

        for q in range(PIECES):
            forward(0, q)
        for j in (1, 2, 3):
            for q in range(PIECES):
                arrived(up[j][q : q + 1])
                go(mate[j][q : q + 1])
                go(cross[j][q : q + 1])
                behind.append((j, q))
                if len(behind) > BEHIND:
                    forward(*behind.pop(0))
        for q in range(PIECES):
            arrived(cross[SHARED][q : q + 1])
            go(cross[4 + SHARED][q : q + 1])
        for j, q in behind:
            forward(j, q)
        for u in (0, 4, 1, 5):
            arrived(cross[u])
        ffn(r, par, 0, 4 * CAP, psend)
        go(back[5])
        go(back[1])
        go(back[4])
        if r == 0:
            handoff_over()
        ffn(r, own, 0, 8 * CAP, pown)
        ms[r, 0] = pown[unit(4), :].astype(BF16)
        go(pair[0])
        for u in (6, 3, 7):
            arrived(cross[u])
        ffn(r, par, 4 * CAP, 4 * CAP, psend)
        for u in (7, 3, 6, 2):
            go(back[u])
        arrived(back[4])
        psend[r, unit(0), :] = (psend[r, unit(0), :].astype(F32) + ppr[r].astype(F32)).astype(BF16)
        go(back[0])
        if r == 0:
            handoff[0].wait_recv()
            handoff[1].wait_recv()
            coef[0] = split_coefs(routing(pids[...], pwts[...], experts)[1])

        def toward_mate(j):
            for q in range(PIECES):
                arrived(back[4 + j][q : q + 1])
                mine, got = pown[unit(4 + j), piece(q)], rx[r, unit(4 + j), piece(q)]
                ms[r, j, :, piece(q)] = (mine + got.astype(F32)).astype(BF16)
                go(pair[j][q : q + 1])

        def finish(j):
            for q in range(PIECES):
                arrived(back[j][q : q + 1])
                arrived(pair[j][q : q + 1])
                mine, got = pown[unit(j), piece(q)], rx[r, unit(j), piece(q)]
                summed = mine + got.astype(F32) + rz[r, j, :, piece(q)].astype(F32)
                fs[r, j, :, piece(q)] = summed.astype(BF16)
                go(last[j][q : q + 1], tracked=r == 0 or j > 0)

        toward_mate(1)
        toward_mate(3)
        finish(1)
        toward_mate(2)
        if r == 0:
            handoff_home()
        finish(3)

        finish(2)
        finish(0)
        if r == 0:
            for j in (1, 3, 2, 0):
                arrived(last[j])
            handoff_arrived()
            epilogue()
            keep_base.start()
        else:
            for copy in started[: -2 * PIECES] + handoff:
                copy.wait_send()
            handoff_sent()
            keep_coefs.wait()
            keep_base.wait()
            for j in (1, 3, 2):
                arrived(last[j])
            for copy in last[0]:
                copy.wait()

    for copy in started[-2 * PIECES :]:
        copy.wait_send()


def body(activations, norm_gain, w_gate, w_up, w_down, expert_ids, route_weights):
    tokens, width = activations.shape[1:]
    hidden = w_gate.shape[2]
    slots = 4 * CAP
    anywhere = pl.BlockSpec(memory_space=pl.ANY)
    vmem = pl.BlockSpec(memory_space=pltpu.VMEM)
    base, results, coefs = pl.pallas_call(
        kernel,
        out_shape=[
            jax.ShapeDtypeStruct((tokens, width), BF16),
            jax.ShapeDtypeStruct((slots, width), BF16),
            jax.ShapeDtypeStruct((tokens, 4 * slots), BF16),
        ],
        in_specs=[anywhere, vmem, anywhere, anywhere, anywhere, vmem, vmem],
        out_specs=[anywhere, anywhere, anywhere],
        scratch_shapes=[
            pltpu.VMEM((3, tokens, width), BF16),
            pltpu.VMEM((2, slots, tokens), BF16),
            pltpu.VMEM((2, tokens, 4 * slots), BF16),
            pltpu.VMEM((slots, width), F32),
            pltpu.VMEM((2, 4, CAP, width), BF16),
            pltpu.VMEM((2, 8 * CAP, width), BF16),
            pltpu.VMEM((2, 8 * CAP, width), BF16),
            pltpu.VMEM((8 * CAP, 2 * hidden), F32),
            pltpu.VMEM((8 * CAP, hidden), BF16),
            pltpu.VMEM((2, 8 * CAP, width), BF16),
            pltpu.VMEM((8 * CAP, width), F32),
            pltpu.VMEM((2, 8 * CAP, width), BF16),
            pltpu.VMEM((2, 4, CAP, width), BF16),
            pltpu.VMEM((2, 4, CAP, width), BF16),
            pltpu.VMEM((2, 4, CAP, width), BF16),
            pltpu.VMEM((slots, width), BF16),
            pltpu.VMEM((width, 2 * hidden), BF16),
            pltpu.VMEM((hidden, width), BF16),
            pltpu.VMEM((8, tokens), jnp.int32),
            pltpu.VMEM((8, tokens), F32),
            pltpu.VMEM((2 * CAP, width), BF16),
            pltpu.VMEM((2, CAP, width), BF16),
            pltpu.SemaphoreType.DMA((2, CHANNELS * PIECES)),
            pltpu.SemaphoreType.DMA((2, CHANNELS * PIECES)),
            pltpu.SemaphoreType.DMA((8,)),
            pltpu.SemaphoreType.DMA((8,)),
            pltpu.SemaphoreType.DMA((6,)),
        ],
        compiler_params=pltpu.CompilerParams(
            collective_id=0, has_side_effects=True, vmem_limit_bytes=56 << 20
        ),
        cost_estimate=pl.CostEstimate(
            flops=12 * 256 * width * hidden, bytes_accessed=12 << 20, transcendentals=512 * hidden
        ),
    )(
        activations[0],
        norm_gain,
        w_gate[0],
        w_up[0],
        w_down[0],
        jnp.swapaxes(expert_ids[:, 0], 1, 2),
        jnp.swapaxes(route_weights[:, 0], 1, 2),
    )
    step = 1024
    pieces = width // step
    return pl.pallas_call(
        last_step,
        out_shape=jax.ShapeDtypeStruct((1, tokens, width), BF16),
        in_specs=[anywhere] * 3,
        out_specs=anywhere,
        scratch_shapes=[
            pltpu.VMEM((tokens, 4 * slots), BF16),
            pltpu.VMEM((pieces, slots, step), BF16),
            pltpu.VMEM((pieces, tokens, step), BF16),
            pltpu.VMEM((pieces, tokens, step), BF16),
            pltpu.SemaphoreType.DMA((2 * pieces + 1,)),
            pltpu.SemaphoreType.DMA((pieces,)),
        ],
        compiler_params=pltpu.CompilerParams(vmem_limit_bytes=56 << 20),
    )(coefs, results, base)


def solution(mesh):
    return jax.shard_map(
        body,
        mesh=mesh,
        in_specs=(
            P("section", "expert", None),
            P("section", None),
            P("section", None, "expert"),
            P("section", None, "expert"),
            P("section", "expert", None),
            P(None, "section", "expert", None),
            P(None, "section", "expert", None),
        ),
        out_specs=P("section", "expert", None),
        check_vma=False,
    )
```

```python
import functools

import jax
import jax.numpy as jnp
from jax import lax
from jax.experimental import pallas as pl
from jax.experimental.pallas import tpu as pltpu
from jax.sharding import PartitionSpec as P

MESH = pl.DeviceIdType.MESH
F32, BF16 = jnp.float32, jnp.bfloat16
POS = {0: 0, 4: 1, 1: 2, 5: 3, 2: 4, 6: 5, 3: 6, 7: 7}
CAP = 16
UP, MATE, CROSS, BACK, PAIR, LAST = 0, 4, 8, 16, 24, 28
CHANNELS = 32
PIECES = 2
SHARED = 2
BEHIND = 3


def unit(u):
    return pl.ds(POS[u] * CAP, CAP)


def routing(ids, weights, experts):
    tokens = ids.shape[1]
    matched, factors = [], []
    for e in experts:
        hit = ids == e
        matched.append(jnp.max(jnp.where(hit, 1.0, 0.0), axis=0, keepdims=True))
        factors.append(jnp.sum(jnp.where(hit, weights, 0.0), axis=0, keepdims=True))
    named = jnp.concatenate(matched + matched, axis=0)
    earlier = lax.broadcasted_iota(jnp.int32, (tokens, tokens), 0) < lax.broadcasted_iota(
        jnp.int32, (tokens, tokens), 1
    )
    rank = jnp.dot(
        named.astype(BF16), jnp.where(earlier, 1.0, 0.0).astype(BF16), preferred_element_type=F32
    )
    slot = lax.broadcasted_iota(jnp.int32, (CAP, tokens), 0).astype(F32)
    select = [
        jnp.where(jnp.logical_and(rank[j : j + 1] == slot, matched[j] > 0.5), 1.0, 0.0)
        for j in range(4)
    ]
    coefs = jnp.concatenate([select[j] * factors[j] for j in range(4)], axis=0)
    return jnp.concatenate(select, axis=0).astype(BF16), coefs


def split_coefs(coefs):
    first = coefs.astype(BF16).astype(F32)
    second = (coefs - first).astype(BF16).astype(F32)
    third = coefs - first - second
    left = jnp.concatenate([first, second], axis=0).T
    right = jnp.concatenate([third, jnp.zeros_like(third)], axis=0).T
    return jnp.concatenate([left, right], axis=1).astype(BF16)


def combine(coefs, results, carried):
    mixed = jnp.dot(coefs, jnp.concatenate([results] * 4, axis=0), preferred_element_type=F32)
    return (carried.astype(F32) + mixed).astype(BF16)


def last_step(coefs, results, carried, out, c, r, t, o, sems, osems):
    step = r.shape[2]
    loads = [pltpu.make_async_copy(coefs, c, sems.at[0])]
    for n in range(r.shape[0]):
        cols = pl.ds(n * step, step)
        loads.append(pltpu.make_async_copy(results.at[:, cols], r.at[n], sems.at[2 * n + 1]))
        loads.append(pltpu.make_async_copy(carried.at[:, cols], t.at[n], sems.at[2 * n + 2]))
    for load in loads:
        load.start()
    loads[0].wait()
    stores = []
    for n in range(r.shape[0]):
        loads[2 * n + 1].wait()
        loads[2 * n + 2].wait()
        o[n] = combine(c[...], r[n], t[n])
        stores.append(pltpu.make_async_copy(o.at[n], out.at[0, :, pl.ds(n * step, step)], osems.at[n]))
        stores[n].start()
    for store in stores:
        store.wait()


def kernel(
    act, gain, wg, wu, wd, ids, weights, base, results, coefs1,
    tok, sel, coef, rows, sbuf, own, par, gu, hid, psend, pown, rx, ms, rz, fs, res, w1, w2, pids, pwts,
    relay, ppr, ssem, rsem, hs, hr, lsem,
):
    s, k = lax.axis_index("section"), lax.axis_index("expert")
    sections = lax.axis_size("section")
    z, h = k // 2, lax.rem(k, 2)
    b = lax.rem(z, 2)
    dr = 2 * b - 1
    p = z // 2
    width = tok.shape[2]
    hidden = wd.shape[0]
    nxt, prv = lax.rem(s + 1, sections), lax.rem(s + sections - 1, sections)

    def at(dz=0, cross=False, section=None):
        there = lax.rem(z + dz + 8, 8) * 2 + (1 - h if cross else h)
        return (s if section is None else section, there)

    loads = [
        pltpu.make_async_copy(act, tok.at[0], lsem.at[0]),
        pltpu.make_async_copy(wg, w1.at[:, pl.ds(0, hidden)], lsem.at[1]),
        pltpu.make_async_copy(wu, w1.at[:, pl.ds(hidden, hidden)], lsem.at[2]),
        pltpu.make_async_copy(wd, w2, lsem.at[3]),
    ]
    for load in loads:
        load.start()
    keep_coefs = pltpu.make_async_copy(coef.at[1], coefs1, lsem.at[4])
    keep_base = pltpu.make_async_copy(tok.at[2], base, lsem.at[5])

    barrier = pltpu.get_barrier_semaphore()
    near = [at(dr), at(2 * dr), at(-2 * dr), at(3 * dr), at(-dr), at(0, cross=True)]
    below = [at(j, section=prv) for j in (0, dr, -2 * dr, 3 * dr)]
    for device in near + below:
        pl.semaphore_signal(barrier, inc=1, device_id=device, device_id_type=MESH)

    side, y, core = s // 8, lax.rem(s // 2, 4), lax.rem(s, 2)
    tail, head = side * 8 + 7, (1 - side) * 8
    is_tail = jnp.logical_and(y == 3, core == 1)
    is_head = jnp.logical_and(y == 0, core == 0)
    before = jnp.logical_and(y < 3, core == 1)
    after = jnp.logical_and(y > 0, core == 0)

    def greet(section):
        pl.semaphore_signal(barrier, inc=1, device_id=at(section=section), device_id_type=MESH)

    @pl.when(before)
    def _():
        greet(tail)

    @pl.when(after)
    def _():
        greet(jnp.where(y == 3, head + 7, head + 2 * y + 1))

    @pl.when(is_head)
    def _():
        greet(head + 1)
        for q in (1, 2, 3):
            greet(side * 8 + 2 * q)

    more = jnp.where(is_tail, 4, jnp.where(is_head, 0, 1))

    def remote(src, dst, send, recv, device):
        return pltpu.make_async_remote_copy(
            src_ref=src, dst_ref=dst, send_sem=send, recv_sem=recv, device_id=device, device_id_type=MESH
        )

    handoff = [
        remote(ids.at[0], pids, hs.at[0], hr.at[0], at(section=nxt)),
        remote(weights.at[0], pwts, hs.at[1], hr.at[1], at(section=nxt)),
    ]
    whole = remote(act, tok.at[1], hs.at[2], hr.at[2], at(section=nxt))

    def quarter(q):
        return pl.ds(q * 2 * CAP, 2 * CAP)

    parts = [
        remote(
            act.at[quarter(q)], relay, hs.at[3 + q], hr.at[3],
            at(section=side * 8 + 2 * q + 1 if q < 3 else head + 6),
        )
        for q in range(4)
    ]
    over = remote(relay, relay, hs.at[7], hr.at[3], at(section=head + 2 * y))
    over_last = remote(relay, tok.at[1, quarter(0)], hs.at[7], hr.at[4], at(section=head))
    home = [
        remote(relay, tok.at[1, quarter(q)], hs.at[7], hr.at[4 + q], at(section=side * 8))
        for q in range(1, 4)
    ]

    def handoff_start():
        @pl.when(is_tail)
        def _():
            for copy in parts:
                copy.start()

        @pl.when(jnp.logical_not(is_tail))
        def _():
            whole.start()

    def handoff_over():
        @pl.when(before)
        def _():
            over.wait_recv()

            @pl.when(y == 0)
            def _():
                over_last.start()

            @pl.when(y > 0)
            def _():
                over.start()

    def handoff_home():
        @pl.when(after)
        def _():
            over.wait_recv()
            for q in range(1, 4):

                @pl.when(y == q)
                def _():
                    home[q - 1].start()

    def handoff_arrived():
        @pl.when(is_head)
        def _():
            over_last.wait_recv()
            for copy in home:
                copy.wait_recv()

        @pl.when(jnp.logical_not(is_head))
        def _():
            whole.wait_recv()

    def handoff_sent():
        @pl.when(is_tail)
        def _():
            for copy in parts:
                copy.wait_send()

        @pl.when(jnp.logical_not(is_tail))
        def _():
            whole.wait_send()

        @pl.when(jnp.logical_or(before, after))
        def _():
            over.wait_send()
    experts = (p, lax.rem(p + dr + 4, 4), lax.rem(p - dr + 4, 4), lax.rem(p + 2, 4))
    sel[0] = routing(ids[0], weights[0], experts)[0]
    loads[0].wait()

    def prologue(r):
        total = jnp.zeros((4 * CAP, 128), F32)
        for n in range(0, width, 1024):
            cols = pl.ds(n, 1024)
            block = jnp.dot(sel[r], tok[2 * r, :, cols], preferred_element_type=F32)
            rows[:, cols] = block
            for m in range(0, 1024, 128):
                total += block[:, m : m + 128] * block[:, m : m + 128]
        scale = lax.rsqrt(jnp.sum(total, axis=1, keepdims=True) * (1.0 / width) + 1e-06)
        for n in range(0, width, 1024):
            cols = pl.ds(n, 1024)
            block = (rows[:, cols] * scale * gain[:, cols].astype(F32)).astype(BF16)
            own[r, unit(0), cols] = block[:CAP]
            for j in range(1, 4):
                sbuf[r, j, :, cols] = block[j * CAP : (j + 1) * CAP]

    def epilogue():
        for n in range(0, width, 1024):
            cols = pl.ds(n, 1024)
            tok[2, :, cols] = combine(coef[0], res[:, cols], tok[1, :, cols])

    def ffn(r, table, start, count, dst):
        chunk = pl.ds(start, count)

        @pl.loop(0, (2 * hidden) // 256)
        def _(n):
            cols = pl.ds(pl.multiple_of(n * 256, 256), 256)
            gu[pl.ds(0, count), cols] = jnp.dot(
                table[r, chunk, :], w1[:, cols], preferred_element_type=F32
            )

        gate, up = gu[pl.ds(0, count), pl.ds(0, hidden)], gu[pl.ds(0, count), pl.ds(hidden, hidden)]
        hid[pl.ds(0, count), :] = (gate / (1.0 + jnp.exp(-gate)) * up).astype(BF16)

        for n in range(0, width, 1024):
            cols = pl.ds(n, 1024)
            block = jnp.dot(hid[pl.ds(0, count), :], w2[:, cols], preferred_element_type=F32)
            if dst is pown:
                dst[chunk, cols] = block
            else:
                dst[r, chunk, cols] = block.astype(BF16)

    started = []

    def piece(q):
        return pl.ds(q * (width // PIECES), width // PIECES)

    for r in range(2):

        def channel(src, dst, index, device):
            return [
                remote(
                    src.at[:, piece(q)], dst.at[:, piece(q)],
                    ssem.at[r, index * PIECES + q], rsem.at[r, index * PIECES + q], device,
                )
                for q in range(PIECES)
            ]

        up = {
            j: channel(sbuf.at[r, j], own.at[r, unit(j)], UP + j, at(d))
            for j, d in ((1, dr), (2, -2 * dr), (3, 3 * dr))
        }
        mate = {
            j: channel(own.at[r, unit(j)], own.at[r, unit(4 + j)], MATE + j, at(-dr))
            for j in range(4)
        }
        cross = {
            u: channel(own.at[r, unit(u)], par.at[r, unit(u)], CROSS + u, at(0, cross=True))
            for u in range(8)
            if u != 4 + SHARED
        }
        cross[4 + SHARED] = channel(
            par.at[r, unit(SHARED)], par.at[r, unit(4 + SHARED)], CROSS + 4 + SHARED, at(-dr)
        )
        back = {
            u: channel(psend.at[r, unit(u)], rx.at[r, unit(u)], BACK + u, at(0, cross=True))
            for u in (0, 1, 2, 3, 5, 6, 7)
        }
        back[4] = channel(psend.at[r, unit(4)], ppr.at[r], BACK + 4, at(-dr))
        pair = {
            j: channel(ms.at[r, j], rz.at[r, j], PAIR + j, at(-dr)) for j in range(4)
        }
        dest, target = (res, nxt) if r == 0 else (results, s)
        last = {
            j: channel(
                fs.at[r, j], dest.at[pl.ds(j * CAP, CAP)], LAST + j, at(dr * j, section=target)
            )
            for j in range(r, 4)
        }
        if r == 1:
            last[0] = [
                pltpu.make_async_copy(
                    fs.at[r, 0, :, piece(q)],
                    results.at[pl.ds(0, CAP), piece(q)],
                    rsem.at[r, LAST * PIECES + q],
                )
                for q in range(PIECES)
            ]

        def go(copies, tracked=True):
            for copy in copies:
                copy.start()
                if tracked:
                    started.append(copy)

        def arrived(copies):
            for copy in copies:
                copy.wait_recv()

        prologue(r)
        if r == 0:
            pl.semaphore_wait(barrier, len(near) + len(below) + more)
        for q in range(PIECES):
            go(cross[0][q : q + 1])
            go(mate[0][q : q + 1])
        for j in (1, 2, 3):
            go(up[j])
        if r == 0:
            for copy in handoff:
                copy.start()
            sel[1], coefs = routing(ids[1], weights[1], experts)
            coef[1] = split_coefs(coefs)
            keep_coefs.start()
            for load in loads[1:]:
                load.wait()
        behind = []

        def forward(j, q):
            arrived(mate[j][q : q + 1])
            if j != SHARED:
                go(cross[4 + j][q : q + 1])

        for q in range(PIECES):
            forward(0, q)
        for j in (1, 2, 3):
            for q in range(PIECES):
                arrived(up[j][q : q + 1])
                go(mate[j][q : q + 1])
                go(cross[j][q : q + 1])
                behind.append((j, q))
                if len(behind) > BEHIND:
                    forward(*behind.pop(0))
        for q in range(PIECES):
            arrived(cross[SHARED][q : q + 1])
            go(cross[4 + SHARED][q : q + 1])
        for j, q in behind:
            forward(j, q)
        if r == 0:
            handoff_start()
        for u in (0, 4, 1, 5):
            arrived(cross[u])
        ffn(r, par, 0, 4 * CAP, psend)
        go(back[5])
        go(back[1])
        go(back[4])
        ffn(r, own, 0, 8 * CAP, pown)
        ms[r, 0] = pown[unit(4), :].astype(BF16)
        go(pair[0])
        for u in (6, 3, 7):
            arrived(cross[u])
        ffn(r, par, 4 * CAP, 4 * CAP, psend)
        for u in (7, 3, 6, 2):
            go(back[u])
        arrived(back[4])
        psend[r, unit(0), :] = (psend[r, unit(0), :].astype(F32) + ppr[r].astype(F32)).astype(BF16)
        go(back[0])
        if r == 0:
            handoff[0].wait_recv()
            handoff[1].wait_recv()
            coef[0] = split_coefs(routing(pids[...], pwts[...], experts)[1])
            handoff_over()

        def toward_mate(j):
            for q in range(PIECES):
                arrived(back[4 + j][q : q + 1])
                mine, got = pown[unit(4 + j), piece(q)], rx[r, unit(4 + j), piece(q)]
                ms[r, j, :, piece(q)] = (mine + got.astype(F32)).astype(BF16)
                go(pair[j][q : q + 1])

        def finish(j):
            for q in range(PIECES):
                arrived(back[j][q : q + 1])
                arrived(pair[j][q : q + 1])
                mine, got = pown[unit(j), piece(q)], rx[r, unit(j), piece(q)]
                summed = mine + got.astype(F32) + rz[r, j, :, piece(q)].astype(F32)
                fs[r, j, :, piece(q)] = summed.astype(BF16)
                go(last[j][q : q + 1], tracked=r == 0 or j > 0)

        toward_mate(1)
        toward_mate(3)
        finish(1)
        toward_mate(2)
        if r == 0:
            handoff_home()
        finish(3)

        finish(2)
        finish(0)
        if r == 0:
            for j in (1, 3, 2, 0):
                arrived(last[j])
            handoff_arrived()
            epilogue()
            keep_base.start()
        else:
            for copy in started[: -2 * PIECES] + handoff:
                copy.wait_send()
            handoff_sent()
            keep_coefs.wait()
            keep_base.wait()
            for j in (1, 3, 2):
                arrived(last[j])
            for copy in last[0]:
                copy.wait()

    for copy in started[-2 * PIECES :]:
        copy.wait_send()


def body(activations, norm_gain, w_gate, w_up, w_down, expert_ids, route_weights):
    tokens, width = activations.shape[1:]
    hidden = w_gate.shape[2]
    slots = 4 * CAP
    anywhere = pl.BlockSpec(memory_space=pl.ANY)
    vmem = pl.BlockSpec(memory_space=pltpu.VMEM)
    base, results, coefs = pl.pallas_call(
        kernel,
        out_shape=[
            jax.ShapeDtypeStruct((tokens, width), BF16),
            jax.ShapeDtypeStruct((slots, width), BF16),
            jax.ShapeDtypeStruct((tokens, 4 * slots), BF16),
        ],
        in_specs=[anywhere, vmem, anywhere, anywhere, anywhere, vmem, vmem],
        out_specs=[anywhere, anywhere, anywhere],
        scratch_shapes=[
            pltpu.VMEM((3, tokens, width), BF16),
            pltpu.VMEM((2, slots, tokens), BF16),
            pltpu.VMEM((2, tokens, 4 * slots), BF16),
            pltpu.VMEM((slots, width), F32),
            pltpu.VMEM((2, 4, CAP, width), BF16),
            pltpu.VMEM((2, 8 * CAP, width), BF16),
            pltpu.VMEM((2, 8 * CAP, width), BF16),
            pltpu.VMEM((8 * CAP, 2 * hidden), F32),
            pltpu.VMEM((8 * CAP, hidden), BF16),
            pltpu.VMEM((2, 8 * CAP, width), BF16),
            pltpu.VMEM((8 * CAP, width), F32),
            pltpu.VMEM((2, 8 * CAP, width), BF16),
            pltpu.VMEM((2, 4, CAP, width), BF16),
            pltpu.VMEM((2, 4, CAP, width), BF16),
            pltpu.VMEM((2, 4, CAP, width), BF16),
            pltpu.VMEM((slots, width), BF16),
            pltpu.VMEM((width, 2 * hidden), BF16),
            pltpu.VMEM((hidden, width), BF16),
            pltpu.VMEM((8, tokens), jnp.int32),
            pltpu.VMEM((8, tokens), F32),
            pltpu.VMEM((2 * CAP, width), BF16),
            pltpu.VMEM((2, CAP, width), BF16),
            pltpu.SemaphoreType.DMA((2, CHANNELS * PIECES)),
            pltpu.SemaphoreType.DMA((2, CHANNELS * PIECES)),
            pltpu.SemaphoreType.DMA((8,)),
            pltpu.SemaphoreType.DMA((8,)),
            pltpu.SemaphoreType.DMA((6,)),
        ],
        compiler_params=pltpu.CompilerParams(
            collective_id=0, has_side_effects=True, vmem_limit_bytes=56 << 20
        ),
        cost_estimate=pl.CostEstimate(
            flops=12 * 256 * width * hidden, bytes_accessed=12 << 20, transcendentals=512 * hidden
        ),
    )(
        activations[0],
        norm_gain,
        w_gate[0],
        w_up[0],
        w_down[0],
        jnp.swapaxes(expert_ids[:, 0], 1, 2),
        jnp.swapaxes(route_weights[:, 0], 1, 2),
    )
    step = 1024
    pieces = width // step
    return pl.pallas_call(
        last_step,
        out_shape=jax.ShapeDtypeStruct((1, tokens, width), BF16),
        in_specs=[anywhere] * 3,
        out_specs=anywhere,
        scratch_shapes=[
            pltpu.VMEM((tokens, 4 * slots), BF16),
            pltpu.VMEM((pieces, slots, step), BF16),
            pltpu.VMEM((pieces, tokens, step), BF16),
            pltpu.VMEM((pieces, tokens, step), BF16),
            pltpu.SemaphoreType.DMA((2 * pieces + 1,)),
            pltpu.SemaphoreType.DMA((pieces,)),
        ],
        compiler_params=pltpu.CompilerParams(vmem_limit_bytes=56 << 20),
    )(coefs, results, base)


def solution(mesh):
    return jax.shard_map(
        body,
        mesh=mesh,
        in_specs=(
            P("section", "expert", None),
            P("section", None),
            P("section", None, "expert"),
            P("section", None, "expert"),
            P("section", "expert", None),
            P(None, "section", "expert", None),
            P(None, "section", "expert", None),
        ),
        out_specs=P("section", "expert", None),
        check_vma=False,
    )
```
